256 devices in a mesh: tm: 16 (over y, z_lo, core), space: 16 (over x, z_hi).
Axes of the slice: x: 4, y: 4, z: 8 (z_hi: 4, z_lo: 2; z = z_hi * 2 + z_lo), core: 2. Of those that a mesh axis runs over, the one named last changes fastest.
Arguments:
- checkpoints: float32 [16, 64, 128, 128], P('tm', 'space'), may hold values from -1 to 1
- guess: float32 [16, 64, 128, 128], P('tm', 'space'), may hold values from -6 to 6
- materials: int32 [64, 128, 128], P('space'), may hold values from 0 to 7
- table: float32 [8], replicated, may hold values from 0.5 to 2
- weight: float32 [64, 128, 128], P('space'), may hold values from 0.2 to 2
Outputs:
- corrected: float32 [16, 64, 128, 128], P('tm', 'space')
- sensitivity: float32 [64, 128, 128], P('space', None, 'tm')
The draws below stay inside these ranges and needn't reach their ends.
All inputs are finite; a program needn't handle non-finite values.
Results may differ from the reference program's by a relative error of at most 0.00002.
Values sent between devices are 32-bit elements; how exact they have to be, the bound alone decides.
A program may use at most 128 MiB of HBM per device.

```python
import math
import jax
import jax.numpy as jnp
from jax import lax

NY = 128
NZ = 128
COARSEN = 8
MATS = 8
NX = 64
NC = 16


def plant(values, rng, low, high):
    dims = values.shape
    spot = [jax.random.randint(jax.random.fold_in(rng, axis), (), 0, dims[axis]) for axis in range(len(dims))]
    values = values.at[tuple(spot)].set(low)
    longest = dims.index(max(dims))
    spot[longest] = (spot[longest] + 1) % dims[longest]
    return values.at[tuple(spot)].set(high)


def block_scale(rng, dims, split, low, high):
    factor_of = 1.0
    for position, blocks in split:
        steps = jax.random.uniform(jax.random.fold_in(jax.random.fold_in(rng, 6), position), (blocks,), jnp.float32, low / len(split), high / len(split))
        factor_of = factor_of * jnp.repeat(jnp.exp(steps), dims[position] // blocks).reshape((-1,) + (1,) * (len(dims) - 1 - position))
    return factor_of


def noise(own_key, dims, scale, most, pieces=(), held_as=jnp.bfloat16):
    values = scale * jax.random.normal(own_key, dims, jnp.float32)
    if pieces:
        values = values * block_scale(own_key, dims, pieces, -0.22, 0.18)
    return jnp.clip(values, -most, most).astype(held_as)


def setup_inputs(seed: int = 0) -> dict:
    arg_keys = jax.random.split(jax.random.key(seed), 6)
    return {
        "checkpoints": jnp.clip(jax.random.uniform(arg_keys[0], (NC, NX, NY, NZ), jnp.float32, -1.0, 1.0) * block_scale(arg_keys[0], (NC, NX, NY, NZ), ((0, 16), (1, 16)), -0.4, 0.0), -1.0, 1.0),
        "guess": noise(arg_keys[1], (NC, NX, NY, NZ), 1.0, 6.0, ((0, 16), (1, 16)), jnp.float32),
        "materials": plant(jax.random.randint(arg_keys[2], (NX, NY, NZ), 0, MATS), jax.random.fold_in(arg_keys[2], 1), 0, MATS - 1).astype(jnp.int32),
        "table": jnp.clip(jnp.exp(jax.random.uniform(arg_keys[3], (MATS,), jnp.float32, math.log(0.5), math.log(2.0))), 0.5, 2.0),
        "weight": jnp.clip(jnp.exp(math.log(2.0) - 2.3025851 * jax.random.uniform(arg_keys[4], (NX, NY, NZ), jnp.float32) ** block_scale(arg_keys[4], (NX, NY, NZ), ((0, 16),), -0.2, 0.2)), 0.2, 2.0),
    }


fine_rate = 0.006
conduct_slope = 0.5


def widen(field):
    return jnp.pad(field, [(0, 0)] * (field.ndim - 2) + [(1, 1), (1, 1)])


def pad_planes(field):
    return jnp.pad(field, [(0, 0)] * (field.ndim - 3) + [(1, 1), (0, 0), (0, 0)])


def neighbours(padded):
    centre = padded[..., 1:-1, 1:-1, 1:-1]
    beside_all = [padded[..., 2:, 1:-1, 1:-1], padded[..., :-2, 1:-1, 1:-1],
              padded[..., 1:-1, 2:, 1:-1], padded[..., 1:-1, :-2, 1:-1],
              padded[..., 1:-1, 1:-1, 2:], padded[..., 1:-1, 1:-1, :-2]]
    return centre, beside_all


def conductivity(materials, table):
    result = jnp.zeros(materials.shape, jnp.float32)
    for number in range(table.shape[0]):
        result = result + jnp.where(materials == number, table[number], 0.0)
    return result


def forward_step(temp_ext, base_ext):
    heat, heat_side = neighbours(widen(temp_ext))
    conduct, conduct_side = neighbours(widen(base_ext * (1.0 + conduct_slope * temp_ext)))
    flow = jnp.zeros_like(heat)
    for other_heat, other_cond in zip(heat_side, conduct_side):
        flow = flow + 0.5 * (conduct + other_cond) * (other_heat - heat)
    return heat + fine_rate * flow


def adjoint_step(adjoint_ext, temp_ext, base_ext, factor):
    latest, latest_side = neighbours(widen(adjoint_ext))
    heat, heat_side = neighbours(widen(temp_ext))
    conduct, conduct_side = neighbours(widen(base_ext * (1.0 + conduct_slope * temp_ext)))
    base_mid = base_ext[..., 1:-1, :, :]
    flow = jnp.zeros_like(latest)
    spread = jnp.zeros_like(latest)
    for other_adj, other_heat, other_cond in zip(latest_side, heat_side, conduct_side):
        flow = flow + 0.5 * (conduct + other_cond) * (other_adj - latest)
        spread = spread + (other_heat - heat) * (latest - other_adj)
    return latest + factor * flow + 0.5 * factor * conduct_slope * base_mid * spread, spread


def reference(checkpoints, guess, materials, table, weight):
    base = conductivity(materials, table)
    base_ext = pad_planes(base)
    zero_field = jnp.zeros_like(guess[:1])

    def history(start):
        states = [start]
        for offset in range(COARSEN - 1):
            states.append(forward_step(pad_planes(states[-1]), base_ext))
        return states

    def relax(pair):
        start, after = pair
        states = history(start)
        latest = after
        for offset in reversed(range(COARSEN)):
            stepped = adjoint_step(pad_planes(latest), pad_planes(states[offset]), base_ext, fine_rate)[0]
            latest = stepped + weight * states[offset]
        return latest

    upcoming = jnp.concatenate([guess[1:], zero_field], 0)
    relaxed = lax.map(relax, (checkpoints, upcoming))
    residual = relaxed - guess

    def descend(error, pair):
        temp, source = pair
        error = adjoint_step(pad_planes(error), pad_planes(temp), base_ext, COARSEN * fine_rate)[0] + source
        return error, error

    _, errors = lax.scan(descend, jnp.zeros_like(guess[0]), (checkpoints, residual), reverse=True)
    corrected = guess + errors

    def finish(pair):
        start, after = pair
        states = history(start)
        latest = after
        total = jnp.zeros_like(start)
        for offset in reversed(range(COARSEN)):
            stepped, spread = adjoint_step(pad_planes(latest), pad_planes(states[offset]), base_ext, fine_rate)
            total = total + 0.5 * fine_rate * (1.0 + conduct_slope * states[offset]) * spread
            latest = stepped + weight * states[offset]
        return total

    following = jnp.concatenate([corrected[1:], zero_field], 0)
    sensitivity = jnp.sum(lax.map(finish, (checkpoints, following)), 0)
    return corrected, sensitivity
```

```python
import functools

import jax
import jax.numpy as jnp
from jax import lax
from jax.experimental import pallas as pl
from jax.experimental.pallas import tpu as pltpu
from jax.sharding import PartitionSpec as P

MESH = pl.DeviceIdType.MESH
F32 = jnp.float32

RATE = 0.006
SLOPE = 0.5
LEVELS = 8
Q, PLANES, ROWS, LANES = 4, 8, 16, 128
PADP, PADR = PLANES + 2, 32
MID_P = pl.ds(1, PLANES)
MID_R = pl.ds(8, ROWS)
XM, XP, YM, YP = range(4)


def kernel(
    ck, guess, mats, table, weight,
    out, sens_out,
    st, yh, ys, coef, base_src, bb, by, bp, kb, g, wt, res, cor, err, ey, ep, total, turned, sr, s2, sf,
    barrier_pad,
    ck_send, ck_recv, gu_send, gu_recv, bs_send, bs_recv, wt_send, wt_recv,
    bx_send, bx_recv, ex_send, ex_recv, hop_send, hop_recv, ch_send, ch_recv,
    ce_send, ce_recv, co_send, co_recv, r1_send, r1_recv, r2_send, r2_recv,
):
    t, s = lax.axis_index("tm"), lax.axis_index("space")
    y, zl, c = t // 4, (t // 2) % 2, t % 2
    x, zh = s // 4, s % 4
    z = zh * 2 + zl
    px = x * 2 + c
    mine = zl * 2 + c
    half = zh % 2

    def dev(px_, y_, z_):
        return {"tm": y_ * 4 + (z_ % 2) * 2 + px_ % 2, "space": (px_ // 2) * 4 + z_ // 2}

    near = [
        (px > 0, px - 1, z),
        (px < 7, px + 1, z),
        (z > 0, px, z - 1),
        (z < 7, px, z + 1),
    ]

    barrier = pltpu.get_barrier_semaphore()

    def greet(px_, y_, z_):
        pl.semaphore_signal(barrier, inc=1, device_id=dev(px_, y_, z_), device_id_type=MESH)

    def ring(i, count):
        z_, px_ = i // 2, x * 2 + i % 2
        other = jnp.logical_or(z_ != z, px_ != px)

        @pl.when(other)
        def _():
            greet(px_, y, z_)

        return count

    lax.fori_loop(0, 16, ring, 0)
    count = jnp.int32(15)
    far_ok = jnp.where(c == 0, px > 0, px < 7)
    far = jnp.where(c == 0, px - 1, px + 1)

    @pl.when(far_ok)
    def _():
        greet(far, y, z)

    count = count + far_ok.astype(jnp.int32)

    for dy in range(1, 4):
        y_ = (y + dy) % 4
        greet(px, y_, z)
    count = count + 3
    for dy in (-1, 1):
        y_ok = jnp.logical_and(y + dy >= 0, y + dy < 4)
        for ok, px_, z_ in near:
            both = jnp.logical_and(ok, y_ok)

            @pl.when(both)
            def _(px_=px_, z_=z_, dy=dy):
                greet(px_, y + dy, z_)

            count = count + both.astype(jnp.int32)

    def lookup(p, carry):
        ids = mats[p]
        val = jnp.zeros(ids.shape, F32)
        for number in range(8):
            val = val + jnp.where(ids == number, table[number], 0.0)
        base_src[p] = val
        return carry

    lax.fori_loop(0, 4, lookup, 0)

    row_zero = jnp.zeros((ROWS, LANES), F32)
    for side, plane in ((XM, 0), (XP, PADP - 1)):

        @pl.when(jnp.logical_not(near[side][0]))
        def _(plane=plane):
            bb[plane, MID_R] = row_zero
            for i in range(4):
                err[i, plane, MID_R] = row_zero

            def clear(i, carry):
                for q in range(Q):
                    st[i, q, plane, MID_R] = row_zero
                return carry

            lax.fori_loop(0, 3 * LEVELS, clear, 0)

    for side, k in ((YM, 0), (YP, 1)):

        @pl.when(jnp.logical_not(near[side][0]))
        def _(k=k):
            by[k] = jnp.zeros((PLANES, LANES), F32)
            for i in range(4):
                ey[i, k] = jnp.zeros((PLANES, LANES), F32)

            def clear(i, carry):
                yh[i, k] = jnp.zeros((Q * PLANES, LANES), F32)
                return carry

            lax.fori_loop(0, 3 * LEVELS, clear, 0)

    @pl.when(y == 3)
    def _():
        err[0] = jnp.zeros((PADP, PADR, LANES), F32)
        for k in range(2):
            ey[0, k] = jnp.zeros((PLANES, LANES), F32)
        st[LEVELS, 3, MID_P, MID_R] = jnp.zeros((PLANES, ROWS, LANES), F32)

    pl.semaphore_wait(barrier, count)

    def push(src, dst, ssem, rsem, px_, y_, z_):
        here = jnp.logical_and(jnp.logical_and(px_ == px, z_ == z), y_ == y)

        @pl.when(here)
        def _():
            pltpu.make_async_copy(src, dst, rsem).start()

        @pl.when(jnp.logical_not(here))
        def _():
            pltpu.make_async_remote_copy(
                src_ref=src, dst_ref=dst, send_sem=ssem, recv_sem=rsem,
                device_id=dev(px_, y_, z_), device_id_type=MESH,
            ).start()

    def push_done(src, ssem, px_, y_, z_):
        here = jnp.logical_and(jnp.logical_and(px_ == px, z_ == z), y_ == y)

        @pl.when(jnp.logical_not(here))
        def _():
            pltpu.make_async_copy(src, src, ssem).wait()

    def arrived(dst, rsem):
        pltpu.make_async_copy(dst, dst, rsem).wait()

    to_px = x * 2 + zh // 2
    slot = half * 4 + mine

    def cut(ref, z_):
        return ref.at[pl.ds(0, 4), pl.ds(pl.multiple_of(z_ * ROWS, ROWS), ROWS)]

    def send_ck(i, carry):
        z_ = (z + i) % 8
        push(cut(ck.at[0], z_), st.at[0, mine, pl.ds(1 + 4 * half, 4), MID_R], ck_send.at[i], ck_recv.at[slot], to_px, y, z_)
        return carry

    def send_guess(i, carry):
        z_ = (z + i) % 8
        push(cut(guess.at[0], z_), g.at[mine, pl.ds(4 * half, 4)], gu_send.at[i], gu_recv.at[slot], to_px, y, z_)
        return carry

    for i in range(2):
        z_ = 2 * mine + i
        push(cut(base_src, z_), bb.at[pl.ds(1 + 4 * half, 4), MID_R], bs_send.at[i], bs_recv.at[half], to_px, y, z_)
    lax.fori_loop(0, 8, send_ck, 0)
    for i in range(2):
        z_ = 2 * mine + i
        push(cut(weight, z_), wt.at[pl.ds(4 * half, 4)], wt_send.at[i], wt_recv.at[half], to_px, y, z_)

    def faces(plane_src, row_src, plane_dst, row_dst, ssem, rsem, y_, start, wait):
        sides = [
            (XM, plane_src(1), plane_dst(PADP - 1), XP),
            (XP, plane_src(PLANES), plane_dst(0), XM),
            (YM, row_src(0), row_dst(1), YP),
            (YP, row_src(1), row_dst(0), YM),
        ]
        for side, src, dst, lands in sides:
            ok, px_, z_ = near[side]

            @pl.when(ok)
            def _(side=side, src=src, dst=dst, lands=lands, px_=px_, z_=z_):
                copy = pltpu.make_async_remote_copy(
                    src_ref=src, dst_ref=dst, send_sem=ssem(side), recv_sem=rsem(lands),
                    device_id=dev(px_, y_, z_), device_id_type=MESH,
                )
                if start:
                    copy.start()
                if wait:
                    copy.wait_send()

    def landed(plane_dst, row_dst, rsem):
        sides = [(XM, plane_dst(0)), (XP, plane_dst(PADP - 1)), (YM, row_dst(0)), (YP, row_dst(1))]
        for side, dst in sides:

            @pl.when(near[side][0])
            def _(side=side, dst=dst):
                arrived(dst, rsem(side))

    def batch_args(idx, phase):
        par = idx % 2
        plane = lambda p: st.at[idx, pl.ds(0, Q), p, MID_R]
        return (
            plane, lambda k: ys.at[idx, k], plane, lambda k: yh.at[idx, k],
            lambda side: ex_send.at[phase, par, side], lambda side: ex_recv.at[phase, par, side],
        )

    def batch_start(idx, phase):
        def pack(q, carry):
            for k, row in ((0, 8), (1, 8 + ROWS - 1)):
                for p in range(PLANES):
                    ys[idx, k, pl.ds(q * PLANES + p, 1)] = st[idx, q, 1 + p, pl.ds(row, 1)]
            return carry

        lax.fori_loop(0, Q, pack, 0)
        ps, rs, pd, rd, ss, rr = batch_args(idx, phase)
        faces(ps, rs, pd, rd, ss, rr, y, True, False)

    def batch_wait(idx, phase):
        ps, rs, pd, rd, ss, rr = batch_args(idx, phase)
        landed(pd, rd, rr)
        faces(ps, rs, pd, rd, ss, rr, y, False, True)

        def unpack(q, carry):
            for k, row in ((0, 7), (1, 8 + ROWS)):
                for p in range(PLANES):
                    st[idx, q, 1 + p, pl.ds(row, 1)] = yh[idx, k, pl.ds(q * PLANES + p, 1)]
            return carry

        lax.fori_loop(0, Q, unpack, 0)

    for i in range(2):
        arrived(bb.at[pl.ds(1 + 4 * i, 4), MID_R], bs_recv.at[i])
    for p in range(PLANES):
        for k, row in ((0, 8), (1, 8 + ROWS - 1)):
            bp[k, pl.ds(p, 1)] = bb[1 + p, pl.ds(row, 1)]
    base_plane = lambda p: bb.at[p, MID_R]
    base_args = (
        base_plane, lambda k: bp.at[k], base_plane, lambda k: by.at[k],
        lambda side: bx_send.at[side], lambda side: bx_recv.at[side],
    )
    faces(*base_args, y, True, False)

    for i in range(8):
        arrived(st.at[0, i % 4, pl.ds(1 + 4 * (i // 4), 4), MID_R], ck_recv.at[i])
    batch_start(0, 0)

    landed(base_args[2], base_args[3], base_args[5])
    faces(*base_args, y, False, True)
    for p in range(PLANES):
        for k, row in ((0, 7), (1, 8 + ROWS)):
            bb[1 + p, pl.ds(row, 1)] = by[k, pl.ds(p, 1)]
    for i in range(2):
        arrived(wt.at[pl.ds(4 * i, 4)], wt_recv.at[i])

    lane = lax.broadcasted_iota(jnp.int32, (PLANES, ROWS, LANES), 2)
    first, last = lane == 0, lane == LANES - 1

    def beside(ref):
        mid = ref[MID_P, MID_R]
        return mid, [
            ref[pl.ds(0, PLANES), MID_R],
            ref[pl.ds(2, PLANES), MID_R],
            ref[MID_P, pl.ds(7, ROWS)],
            ref[MID_P, pl.ds(9, ROWS)],
            pltpu.roll(mid, 1, 2),
            pltpu.roll(mid, LANES - 1, 2),
        ]

    def clipped(around):
        return around[:4] + [jnp.where(first, 0.0, around[4]), jnp.where(last, 0.0, around[5])]

    def conductivity(j):
        def one(q, carry):
            kb[q] = bb[...] * (1.0 + SLOPE * st[j, q])
            return carry

        lax.fori_loop(0, Q, one, 0)

    def forward(j):
        def one(q, carry):
            u, u_d = beside(st.at[j, q])
            k, k_d = beside(kb.at[q])
            flow = jnp.zeros_like(u)
            for uu, kk in zip(clipped(u_d), clipped(k_d)):
                flow = flow + (k + kk) * (uu - u)
            st[j + 1, q, MID_P, MID_R] = u + (0.5 * RATE) * flow
            return carry

        lax.fori_loop(0, Q, one, 0)

    def coefficients(j):
        def one(q, carry):
            u, u_d = beside(st.at[j, q])
            k, k_d = beside(kb.at[q])
            b = (0.25 * SLOPE * 2.0 * RATE) * bb[MID_P, MID_R]
            gain = (0.5 * RATE) * (1.0 + SLOPE * u)
            w_sum = jnp.zeros_like(u)
            e_sum = jnp.zeros_like(u)
            for n, (uu, kk) in enumerate(zip(clipped(u_d), clipped(k_d))):
                diff = uu - u
                w = (0.5 * RATE) * (k + kk) - b * diff
                e = gain * diff
                w_sum = w_sum + w
                e_sum = e_sum + e
                if n == 4:
                    w, e = jnp.where(first, 0.0, w), jnp.where(first, 0.0, e)
                if n == 5:
                    w, e = jnp.where(last, 0.0, w), jnp.where(last, 0.0, e)
                coef[j, q, 1 + n] = w
                coef[j, q, 8 + n] = e
            coef[j, q, 0] = w_sum
            coef[j, q, 7] = e_sum
            coef[j, q, 14] = wt[...] * u
            return carry

        lax.fori_loop(0, Q, one, 0)

    def hop_copy():
        return pltpu.make_async_remote_copy(
            src_ref=g.at[0], dst_ref=st.at[LEVELS, 3, MID_P, MID_R], send_sem=hop_send, recv_sem=hop_recv,
            device_id=dev(px, (y + 3) % 4, z), device_id_type=MESH,
        )

    def forward_step(j, carry):
        batch_wait(j, 0)
        conductivity(j)

        @pl.when(j < LEVELS - 1)
        def _():
            forward(j)
            batch_start(j + 1, 0)

        @pl.when(j < 4)
        def _():
            send_guess(2 * j, 0)
            send_guess(2 * j + 1, 0)

        @pl.when(j == 5)
        def _():
            for i in range(8):
                arrived(g.at[i % 4, pl.ds(4 * (i // 4), 4)], gu_recv.at[i])

            @pl.when(y > 0)
            def _():
                hop_copy().start()

            for q in range(3):
                st[LEVELS, q, MID_P, MID_R] = g[q + 1]

        @pl.when(j == LEVELS - 1)
        def _():
            @pl.when(y < 3)
            def _():
                hop_copy().wait_recv()

            batch_start(LEVELS, 1)

        coefficients(j)
        return carry

    lax.fori_loop(0, LEVELS, forward_step, 0)

    def apply(ref, j, q, at):
        v, v_d = beside(ref)
        acc = v_d[0] * coef[j, q, at + 1]
        for n in range(1, 6):
            acc = acc + v_d[n] * coef[j, q, at + 1 + n]
        return v, acc - v * coef[j, q, at]

    def adjoint(idx, j):
        def one(q, carry):
            v, change = apply(st.at[idx, q], j, q, 0)
            st[idx + 1, q, MID_P, MID_R] = (v + change) + coef[j, q, 14]
            return carry

        lax.fori_loop(0, Q, one, 0)

    def relax_step(i, carry):
        idx = LEVELS + i
        batch_wait(idx, 1)
        adjoint(idx, LEVELS - 1 - i)

        @pl.when(i < LEVELS - 1)
        def _():
            batch_start(idx + 1, 1)

        return carry

    lax.fori_loop(0, LEVELS, relax_step, 0)

    def residual(q, carry):
        res[q] = st[2 * LEVELS, q, MID_P, MID_R] - g[q]
        return carry

    lax.fori_loop(0, Q, residual, 0)

    def err_args(i, ssem, rsem, to=None):
        to = i if to is None else to
        return (
            lambda p: err.at[i, p, MID_R], lambda k: ep.at[i, k],
            lambda p: err.at[to, p, MID_R], lambda k: ey.at[to, k], ssem, rsem,
        )

    def err_pack(i):
        for p in range(PLANES):
            for k, row in ((0, 8), (1, 8 + ROWS - 1)):
                ep[i, k, pl.ds(p, 1)] = err[i, 1 + p, pl.ds(row, 1)]

    def err_unpack(i):
        for p in range(PLANES):
            for k, row in ((0, 7), (1, 8 + ROWS)):
                err[i, 1 + p, pl.ds(row, 1)] = ey[i, k, pl.ds(p, 1)]

    def cross_args():
        return err_args(4, lambda side: ce_send.at[side], lambda side: ce_recv.at[side], to=0)

    def block_copy():
        return pltpu.make_async_remote_copy(
            src_ref=err.at[4, MID_P, MID_R], dst_ref=err.at[0, MID_P, MID_R], send_sem=ce_send.at[4], recv_sem=ce_recv.at[4],
            device_id=dev(px, (y + 3) % 4, z), device_id_type=MESH,
        )

    def give(q, i, start):
        src = cor.at[q, pl.ds(4 * i, 4)]
        z_, px_ = 2 * (2 * c + i) + q // 2, x * 2 + q % 2
        if start:
            push(src, out.at[0, pl.ds(0, 4), pl.ds(pl.multiple_of(z * ROWS, ROWS), ROWS)], co_send.at[q, i], co_recv.at[z], px_, y, z_)
        else:
            push_done(src, co_send.at[q, i], px_, y, z_)

    for i in range(4):
        q = 3 - i
        if i == 0:

            @pl.when(y < 3)
            def _():
                a = cross_args()
                landed(a[2], a[3], a[5])
                block_copy().wait_recv()

        else:
            a = err_args(i, lambda side, i=i: ch_send.at[i - 1, side], lambda side, i=i: ch_recv.at[i - 1, side])
            landed(a[2], a[3], a[5])
            faces(*a, y, False, True)
        err_unpack(i)
        e, change = apply(err.at[i], 0, q, 0)
        err[i + 1, MID_P, MID_R] = (e + float(LEVELS) * change) + res[q]
        err_pack(i + 1)
        if i < 3:
            a = err_args(i + 1, lambda side, i=i: ch_send.at[i, side], lambda side, i=i: ch_recv.at[i, side])
            faces(*a, y, True, False)
        else:

            @pl.when(y > 0)
            def _():
                block_copy().start()
                faces(*cross_args(), y - 1, True, False)

        st[2 * LEVELS, q] = st[LEVELS, q] + err[i]
        cor[q] = g[q] + err[i + 1, MID_P, MID_R]
        for k in range(2):
            give(q, k, True)

    total[...] = jnp.zeros(total.shape, F32)

    def final_step(i, carry):
        idx = 2 * LEVELS + i
        j = LEVELS - 1 - i

        @pl.when(i > 0)
        def _():
            batch_wait(idx, 2)

        @pl.when(i < LEVELS - 1)
        def _():
            adjoint(idx, j)
            batch_start(idx + 1, 2)

        def one(q, carry):
            _, change = apply(st.at[idx, q], j, q, 7)
            total[...] = total[...] - change
            return carry

        lax.fori_loop(0, Q, one, 0)
        return carry

    lax.fori_loop(0, LEVELS, final_step, 0)

    turned[...] = jnp.transpose(total[...].reshape(PLANES * ROWS, LANES))

    def sum_copy(dy):
        y_ = (y + dy) % 4
        src = turned.at[pl.ds(pl.multiple_of(y_ * 32, 32), 32)]
        return pltpu.make_async_remote_copy(
            src_ref=src, dst_ref=sr.at[dy - 1], send_sem=r1_send.at[dy - 1], recv_sem=r1_recv.at[dy - 1],
            device_id=dev(px, y_, z), device_id_type=MESH,
        )

    for dy in range(1, 4):
        sum_copy(dy).start()
    part = turned[pl.ds(pl.multiple_of(y * 32, 32), 32)]
    for dy in range(1, 4):
        sum_copy(dy).wait_recv()
        part = part + sr[dy - 1]
    s2[0] = part
    s2[1] = pltpu.roll(part, 64, 1)

    def share(n, start):
        i, q = n // 4, n % 4
        src = s2.at[i, pl.ds(8 * q, 8)]
        z_, px_ = 2 * (2 * c + i) + q // 2, x * 2 + q % 2
        if start:
            push(src, sf.at[z], r2_send.at[n], r2_recv.at[z], px_, y, z_)
        else:
            push_done(src, r2_send.at[n], px_, y, z_)

    for n in range(8):
        share(n, True)
    for i in range(8):
        arrived(sf.at[i], r2_recv.at[i])
    sens_out[...] = sf[...]

    for n in range(8):
        share(n, False)
    for dy in range(1, 4):
        sum_copy(dy).wait_send()
    for q in range(4):
        for i in range(2):
            give(q, i, False)
    for i in range(8):
        arrived(out.at[0, pl.ds(0, 4), pl.ds(i * ROWS, ROWS)], co_recv.at[i])

    @pl.when(y > 0)
    def _():
        hop_copy().wait_send()
        block_copy().wait_send()
        faces(*cross_args(), y - 1, False, True)

    for i in range(2):
        z_ = 2 * mine + i
        push_done(cut(base_src, z_), bs_send.at[i], to_px, y, z_)
        push_done(cut(weight, z_), wt_send.at[i], to_px, y, z_)

    def drain(i, carry):
        z_ = (z + i) % 8
        push_done(cut(ck.at[0], z_), ck_send.at[i], to_px, y, z_)
        push_done(cut(guess.at[0], z_), gu_send.at[i], to_px, y, z_)
        return carry

    lax.fori_loop(0, 8, drain, 0)


def on_device(checkpoints, guess, materials, table, weight):
    dma = pltpu.SemaphoreType.DMA
    vmem = lambda *shape: pltpu.VMEM(shape, F32)
    block = (PLANES, ROWS, LANES)
    corrected, shares = pl.pallas_call(
        kernel,
        out_shape=(
            jax.ShapeDtypeStruct(guess.shape, F32),
            jax.ShapeDtypeStruct((8, 8, LANES), F32),
        ),
        in_specs=[
            pl.BlockSpec(memory_space=pl.ANY),
            pl.BlockSpec(memory_space=pl.ANY),
            pl.BlockSpec(memory_space=pltpu.VMEM),
            pl.BlockSpec(memory_space=pltpu.SMEM),
            pl.BlockSpec(memory_space=pl.ANY),
        ],
        out_specs=(
            pl.BlockSpec(memory_space=pl.ANY),
            pl.BlockSpec(memory_space=pltpu.VMEM),
        ),
        scratch_shapes=[
            vmem(3 * LEVELS, Q, PADP, PADR, LANES),
            vmem(3 * LEVELS, 2, Q * PLANES, LANES),
            vmem(3 * LEVELS, 2, Q * PLANES, LANES),
            vmem(LEVELS, Q, 15, *block),
            vmem(4, 128, LANES),
            vmem(PADP, PADR, LANES),
            vmem(2, PLANES, LANES),
            vmem(2, PLANES, LANES),
            vmem(Q, PADP, PADR, LANES),
            vmem(Q, *block),
            vmem(*block),
            vmem(Q, *block),
            vmem(Q, *block),
            vmem(5, PADP, PADR, LANES),
            vmem(5, 2, PLANES, LANES),
            vmem(5, 2, PLANES, LANES),
            vmem(*block),
            vmem(LANES, LANES),
            vmem(3, 32, LANES),
            vmem(2, 32, LANES),
            vmem(8, 8, LANES),
            vmem(8, LANES),
            dma((8,)), dma((8,)), dma((8,)), dma((8,)),
            dma((2,)), dma((2,)), dma((2,)), dma((2,)),
            dma((4,)), dma((4,)),
            dma((3, 2, 4)), dma((3, 2, 4)),
            dma, dma,
            dma((3, 4)), dma((3, 4)),
            dma((5,)), dma((5,)),
            dma((4, 2)), dma((8,)),
            dma((3,)), dma((3,)), dma((8,)), dma((8,)),
        ],
        compiler_params=pltpu.CompilerParams(
            collective_id=0, has_side_effects=True, vmem_limit_bytes=60 * 1024 * 1024
        ),
    )(checkpoints, guess, materials, table, weight)
    parts = shares[:, :, :64].reshape(8, 8, 4, 16)
    sensitivity = jnp.transpose(parts, (2, 0, 3, 1)).reshape(4, 128, 8)
    return corrected, sensitivity


def solution(mesh):
    in_specs = (
        P("tm", "space", None, None),
        P("tm", "space", None, None),
        P("space", None, None),
        P(),
        P("space", None, None),
    )
    out_specs = (P("tm", "space", None, None), P("space", None, "tm"))
    return jax.shard_map(
        on_device, mesh=mesh, in_specs=in_specs, out_specs=out_specs, check_vma=False
    )
```

```python
import functools

import jax
import jax.numpy as jnp
from jax import lax
from jax.experimental import pallas as pl
from jax.experimental.pallas import tpu as pltpu
from jax.sharding import PartitionSpec as P

MESH = pl.DeviceIdType.MESH
F32 = jnp.float32

RATE = 0.006
SLOPE = 0.5
LEVELS = 8
Q, PLANES, ROWS, LANES, H = 4, 8, 16, 128, 4
PADP, PADR = PLANES + 2 * H, ROWS + 2 * H
MID_P, MID_R = pl.ds(H, PLANES), pl.ds(H, ROWS)
SIDES = [(-1, 0), (1, 0), (0, -1), (0, 1), (-1, -1), (1, -1), (-1, 1), (1, 1)]
OPPOSITE = [SIDES.index((-dx, -dz)) for dx, dz in SIDES]
RELAX, FINAL, U2, U6 = 8, 9, 17, 18
EXCHANGED = [0, 3, 7, U2, U6, RELAX, RELAX + 4, RELAX + 8, FINAL, FINAL + 4]
WIDTH = [3, 1, 2, 3, 0, 1, 2, 3]
PLACE = [(3, 1), (2, 1), (1, 1), (0, 1), (3, 0), (2, 0), (1, 0), (0, 0)]
COEF_W = [3, 2, 1, 3]


def chunks(width):
    lo, hi = H - width, H + PLANES + width
    parts = -(-(hi - lo) // 5)
    edges = [lo + (hi - lo) * n // parts for n in range(parts + 1)]
    return list(zip(edges[:-1], edges[1:]))


def kernel(
    ck, guess, mats, table, weight,
    out, sens_out,
    st, yh, ys, c0, c1, c2, c3, base_src, cin, bin_, win, bb, wt, bwh, bws, g, gn, g0, cor, err, ei, eo, eyh, eys,
    total, turned, sr, s2, sf,
    ck_send, ck_recv, gu_send, gu_recv, bs_send, bs_recv, wt_send, wt_recv,
    bx_send, bx_recv, ex_send, ex_recv, hop_send, hop_recv,
    ce_send, ce_recv, co_send, co_recv, r1_send, r1_recv, r2_send, r2_recv,
):
    coef = [c0, c1, c2, c3]
    t, s = lax.axis_index("tm"), lax.axis_index("space")
    y, zl, c = t // 4, (t // 2) % 2, t % 2
    x, zh = s // 4, s % 4
    z = zh * 2 + zl
    px = x * 2 + c
    mine = zl * 2 + c
    half = zh % 2

    def dev(px_, y_, z_):
        return {"tm": y_ * 4 + (z_ % 2) * 2 + px_ % 2, "space": (px_ // 2) * 4 + z_ // 2}

    def there(dx, dz):
        ok = jnp.bool_(True)
        if dx:
            ok = px > 0 if dx < 0 else px < 7
        if dz:
            ok_z = z > 0 if dz < 0 else z < 7
            ok = jnp.logical_and(ok, ok_z) if dx else ok_z
        return ok

    near = [(there(dx, dz), px + dx, z + dz) for dx, dz in SIDES]

    barrier = pltpu.get_barrier_semaphore()

    def greet(px_, y_, z_):
        pl.semaphore_signal(barrier, inc=1, device_id=dev(px_, y_, z_), device_id_type=MESH)

    def ring(i, carry):
        z_, px_ = i // 2, x * 2 + i % 2

        @pl.when(jnp.logical_or(z_ != z, px_ != px))
        def _():
            greet(px_, y, z_)

        return carry

    lax.fori_loop(0, 16, ring, 0)
    count = jnp.int32(15)
    far_ok = jnp.where(c == 0, px > 0, px < 7)
    far = jnp.where(c == 0, px - 1, px + 1)
    for dz in (-1, 0, 1):
        ok = jnp.logical_and(far_ok, there(0, dz)) if dz else far_ok

        @pl.when(ok)
        def _(dz=dz):
            greet(far, y, z + dz)

        count = count + ok.astype(jnp.int32)

    for dy in range(1, 4):
        greet(px, (y + dy) % 4, z)
    count = count + 3
    for dy in (-1, 1):
        y_ok = jnp.logical_and(y + dy >= 0, y + dy < 4)
        for ok, px_, z_ in near:
            both = jnp.logical_and(ok, y_ok)

            @pl.when(both)
            def _(px_=px_, z_=z_, dy=dy):
                greet(px_, y + dy, z_)

            count = count + both.astype(jnp.int32)

    def lookup(p, carry):
        ids = mats[p]
        val = jnp.zeros(ids.shape, F32)
        for number in range(8):
            val = val + jnp.where(ids == number, table[number], 0.0)
        base_src[p] = val
        return carry

    lax.fori_loop(0, 4, lookup, 0)

    for side, lo, rows in ((0, 0, 0), (1, H + PLANES, 48)):

        @pl.when(jnp.logical_not(near[side][0]))
        def _(lo=lo, rows=rows):
            slab = jnp.zeros((H, PADR, LANES), F32)
            for ref in (bb, wt, err.at[0]):
                ref[pl.ds(lo, H)] = slab
            edge = jnp.zeros((16, LANES), F32)
            for k in range(2):
                for n in range(2):
                    bwh[n, k, 0, pl.ds(rows, 16)] = edge
                eyh[k, 0, pl.ds(rows, 16)] = edge

            def clear(q, carry):
                for n, idx in enumerate(EXCHANGED):
                    st[idx, q, pl.ds(lo, H)] = slab
                    for k in range(2):
                        yh[n, k, q, pl.ds(rows, 16)] = edge
                return carry

            lax.fori_loop(0, Q, clear, 0)

    for side, k in ((2, 0), (3, 1)):

        @pl.when(jnp.logical_not(near[side][0]))
        def _(k=k):
            edge = jnp.zeros((64, LANES), F32)
            for n in range(2):
                bwh[n, k, 0] = edge
            eyh[k, 0] = edge

            def clear(q, carry):
                for n in range(len(EXCHANGED)):
                    yh[n, k, q] = edge
                return carry

            lax.fori_loop(0, Q, clear, 0)

    @pl.when(y == 3)
    def _():
        err[0] = jnp.zeros((PADP, PADR, LANES), F32)
        gn[...] = jnp.zeros(gn.shape, F32)

    pl.semaphore_wait(barrier, count)

    def push(src, dst, ssem, rsem, px_, y_, z_):
        here = jnp.logical_and(px_ == px, z_ == z)

        @pl.when(here)
        def _():
            pltpu.make_async_copy(src, dst, rsem).start()

        @pl.when(jnp.logical_not(here))
        def _():
            pltpu.make_async_remote_copy(
                src_ref=src, dst_ref=dst, send_sem=ssem, recv_sem=rsem,
                device_id=dev(px_, y_, z_), device_id_type=MESH,
            ).start()

    def push_done(src, ssem, px_, y_, z_):
        here = jnp.logical_and(px_ == px, z_ == z)

        @pl.when(jnp.logical_not(here))
        def _():
            pltpu.make_async_copy(src, src, ssem).wait()

    def arrived(dst, rsem):
        pltpu.make_async_copy(dst, dst, rsem).wait()

    to_px = x * 2 + zh // 2
    slot = half * 4 + mine

    def cut(ref, z_):
        return ref.at[pl.ds(0, 4), pl.ds(pl.multiple_of(z_ * ROWS, ROWS), ROWS)]

    def send_ck(i, carry):
        z_ = (z + i) % 8
        push(cut(ck.at[0], z_), cin.at[mine, pl.ds(4 * half, 4)], ck_send.at[i], ck_recv.at[slot], to_px, y, z_)
        return carry

    def send_guess(i, carry):
        z_ = (z + i) % 8
        push(cut(guess.at[0], z_), g.at[mine, pl.ds(4 * half, 4)], gu_send.at[i], gu_recv.at[slot], to_px, y, z_)
        return carry

    for i in range(2):
        z_ = 2 * mine + i
        push(cut(base_src, z_), bin_.at[pl.ds(4 * half, 4)], bs_send.at[i], bs_recv.at[half], to_px, y, z_)
    lax.fori_loop(0, 8, send_ck, 0)
    for i in range(2):
        z_ = 2 * mine + i
        push(cut(weight, z_), win.at[pl.ds(4 * half, 4)], wt_send.at[i], wt_recv.at[half], to_px, y, z_)

    def outgoing(field, side):
        planes, rows_out, _ = field
        dx, dz = SIDES[side]
        if dz == 0:
            return planes(H if dx < 0 else PLANES, H)
        k = 0 if dz < 0 else 1
        return rows_out(k, 16 if dx > 0 else 0, 32 if dx == 0 else 16)

    def landing(field, side):
        planes, _, rows_in = field
        dx, dz = SIDES[side]
        if dz == 0:
            return planes(0 if dx < 0 else H + PLANES, H)
        k = 0 if dz < 0 else 1
        return rows_in(k, {0: 16, -1: 0, 1: 48}[dx], 32 if dx == 0 else 16)

    def halo_copy(field, to, side, ssem, rsem, y_):
        _, px_, z_ = near[side]
        back = OPPOSITE[side]
        return pltpu.make_async_remote_copy(
            src_ref=outgoing(field, side), dst_ref=landing(to, back), send_sem=ssem(side), recv_sem=rsem(back),
            device_id=dev(px_, y_, z_), device_id_type=MESH,
        )

    def halo_start(field, to, ssem, rsem, y_):
        for side in (4, 5, 6, 7, 2, 3, 0, 1):

            @pl.when(near[side][0])
            def _(side=side):
                halo_copy(field, to, side, ssem, rsem, y_).start()

    def halo_sent(field, to, ssem, rsem, y_, sides=range(8)):
        for side in sides:

            @pl.when(near[side][0])
            def _(side=side):
                halo_copy(field, to, side, ssem, rsem, y_).wait_send()

    def halo_landed(field, rsem):
        for side in range(8):

            @pl.when(near[side][0])
            def _(side=side):
                arrived(landing(field, side), rsem(side))

    def pack(block, out_rows):
        for p in range(PLANES):
            out_rows[0, pl.ds(4 * p, 4)] = block[H + p, pl.ds(H, 4)]
            out_rows[1, pl.ds(4 * p, 4)] = block[H + p, pl.ds(ROWS, 4)]

    def unpack(block, in_rows):
        for p in range(PADP):
            block[p, pl.ds(0, 4)] = in_rows[0, pl.ds(4 * p, 4)]
            block[p, pl.ds(H + ROWS, 4)] = in_rows[1, pl.ds(4 * p, 4)]

    def batch(idx):
        n = EXCHANGED.index(idx)
        field = (
            lambda lo, m: st.at[idx, pl.ds(0, Q), pl.ds(lo, m)],
            lambda k, lo, m: ys.at[n, k, pl.ds(0, Q), pl.ds(lo, m)],
            lambda k, lo, m: yh.at[n, k, pl.ds(0, Q), pl.ds(lo, m)],
        )
        return n, field, lambda side: ex_send.at[n, side], lambda side: ex_recv.at[n, side]

    def per_q(one):
        def body(q, carry):
            one(q)
            return carry

        lax.fori_loop(0, Q, body, 0)

    def batch_start(idx):
        n, field, ssem, rsem = batch(idx)

        def one(q):
            for p in range(PLANES):
                ys[n, 0, q, pl.ds(4 * p, 4)] = st[idx, q, H + p, pl.ds(H, 4)]
                ys[n, 1, q, pl.ds(4 * p, 4)] = st[idx, q, H + p, pl.ds(ROWS, 4)]

        per_q(one)
        halo_start(field, field, ssem, rsem, y)

    def batch_wait(idx):
        n, field, ssem, rsem = batch(idx)
        halo_landed(field, rsem)
        halo_sent(field, field, ssem, rsem, y, (0, 1))

        def one(q):
            for p in range(PADP):
                st[idx, q, p, pl.ds(0, 4)] = yh[n, 0, q, pl.ds(4 * p, 4)]
                st[idx, q, p, pl.ds(H + ROWS, 4)] = yh[n, 1, q, pl.ds(4 * p, 4)]

        per_q(one)

    def batch_sent(idx):
        n, field, ssem, rsem = batch(idx)
        halo_sent(field, field, ssem, rsem, y, range(2, 8))

    def static_field(n):
        ref = bb if n == 0 else wt
        field = (
            lambda lo, m: ref.at[pl.ds(lo, m)],
            lambda k, lo, m: bws.at[n, k, 0, pl.ds(lo, m)],
            lambda k, lo, m: bwh.at[n, k, 0, pl.ds(lo, m)],
        )
        return field, lambda side: bx_send.at[n, side], lambda side: bx_recv.at[n, side]

    def static_start(n):
        ref, came, sem = (bb, bin_, bs_recv) if n == 0 else (wt, win, wt_recv)
        for i in range(2):
            arrived(came.at[pl.ds(4 * i, 4)], sem.at[i])
        ref[MID_P, MID_R] = came[...]
        pack(ref, bws.at[n, pl.ds(0, 2), 0])
        field, ssem, rsem = static_field(n)
        halo_start(field, field, ssem, rsem, y)

    def static_wait(n):
        field, ssem, rsem = static_field(n)
        halo_landed(field, rsem)
        halo_sent(field, field, ssem, rsem, y, (0, 1))
        unpack(bb if n == 0 else wt, bwh.at[n, pl.ds(0, 2), 0])

    static_start(0)
    for i in range(8):
        arrived(cin.at[i % 4, pl.ds(4 * (i // 4), 4)], ck_recv.at[i])

    def enter(q):
        st[0, q, MID_P, MID_R] = cin[q]

    per_q(enter)
    batch_start(0)
    static_start(1)
    lax.fori_loop(0, 8, send_guess, 0)
    static_wait(0)
    batch_wait(0)

    def edges(n):
        lane = lax.broadcasted_iota(jnp.int32, (n, PADR, LANES), 2)
        return lane == 0, lane == LANES - 1

    def up(a):
        return pltpu.roll(a, PADR - 1, 1)

    def down(a):
        return pltpu.roll(a, 1, 1)

    def right(a):
        return pltpu.roll(a, LANES - 1, 2)

    def left(a):
        return pltpu.roll(a, 1, 2)

    def forward(j, width, copy=None):
        def one(q):
            for lo, hi in chunks(width):
                n = hi - lo
                first, last = edges(n)
                uu = st[j, q, pl.ds(lo - 1, n + 2)]
                base = bb[pl.ds(lo - 1, n + 2)]
                kk = base * (1.0 + SLOPE * uu)
                u, k, b = uu[1:-1], kk[1:-1], base[1:-1]
                f = (kk[1:] + kk[:-1]) * (uu[1:] - uu[:-1])
                flow = f[1:] - f[:-1]
                f = (k + up(k)) * (up(u) - u)
                flow = flow + (f - down(f))
                f = (k + jnp.where(last, 0.0, right(k))) * (jnp.where(last, 0.0, right(u)) - u)
                flow = flow + (f - jnp.where(first, k * u, left(f)))
                new = jnp.where(b > 0.0, u + (0.5 * RATE) * flow, 0.0)
                st[j + 1, q, pl.ds(lo, n)] = new
                if copy is not None:
                    a, z_ = max(lo, H), min(hi, H + PLANES)
                    if a < z_:
                        st[copy, q, pl.ds(a, z_ - a)] = new[a - lo : z_ - lo]

        per_q(one)

    def coefficients(j, field=None):
        idx = j if field is None else field
        array, entry = PLACE[j]
        ref, off = coef[array], H - COEF_W[array]

        def one(q):
            for lo, hi in chunks(WIDTH[j]):
                n = hi - lo
                first, last = edges(n)
                uu = st[idx, q, pl.ds(lo - 1, n + 2)]
                base = bb[pl.ds(lo - 1, n + 2)]
                kk = (0.5 * RATE) * (base * (1.0 + SLOPE * uu))
                u, k = uu[1:-1], kk[1:-1]
                b = (0.25 * RATE) * base[1:-1]
                at = lambda i: (entry, q, i, pl.ds(lo - off, n))
                a, d = kk[1:] + kk[:-1], uu[1:] - uu[:-1]
                less, more = a[:-1] + b * d[:-1], a[1:] - b * d[1:]
                ref[at(1)] = less
                ref[at(2)] = more
                w_sum = less + more
                a, d = k + up(k), up(u) - u
                less, more = down(a) + b * down(d), a - b * d
                ref[at(3)] = less
                ref[at(4)] = more
                w_sum = w_sum + (less + more)
                a, d = k + right(k), right(u) - u
                less, more = left(a) + b * left(d), a - b * d
                ref[at(5)] = jnp.where(first, 0.0, less)
                ref[at(6)] = jnp.where(last, 0.0, more)
                edge = k + b * u
                w_sum = w_sum + (jnp.where(first, edge, less) + jnp.where(last, edge, more))
                ref[at(0)] = w_sum

        per_q(one)

    def change(vv, array, entry, q, lo, n):
        ref, off = coef[array], H - COEF_W[array]
        w = lambda i: ref[entry, q, i, pl.ds(lo - off, n)]
        v = vv[1:-1]
        acc = vv[:-2] * w(1) + vv[2:] * w(2)
        acc = acc + down(v) * w(3)
        acc = acc + up(v) * w(4)
        acc = acc + left(v) * w(5)
        acc = acc + right(v) * w(6)
        return acc - v * w(0)

    def field_of(j):
        return {2: U2, 6: U6}.get(j, j)

    def adjoint(idx, j, width):
        array, entry = PLACE[j]

        def one(q):
            for lo, hi in chunks(width):
                n = hi - lo
                vv = st[idx, q, pl.ds(lo - 1, n + 2)]
                new = (vv[1:-1] + change(vv, array, entry, q, lo, n)) + wt[pl.ds(lo, n)] * st[field_of(j), q, pl.ds(lo, n)]
                st[idx + 1, q, pl.ds(lo, n)] = jnp.where(bb[pl.ds(lo, n)] > 0.0, new, 0.0)

        per_q(one)

    def hop_copy():
        return pltpu.make_async_remote_copy(
            src_ref=g.at[0], dst_ref=gn, send_sem=hop_send, recv_sem=hop_recv,
            device_id=dev(px, (y + 3) % 4, z), device_id_type=MESH,
        )

    forward(0, 2)
    forward(1, 1, copy=U2)
    batch_start(U2)
    forward(2, 0)
    batch_start(3)
    static_wait(1)
    coefficients(0)
    coefficients(1)
    for i in range(8):
        arrived(g.at[i % 4, pl.ds(4 * (i // 4), 4)], gu_recv.at[i])

    @pl.when(y > 0)
    def _():
        hop_copy().start()

    batch_wait(3)
    forward(3, 3)
    forward(4, 2)
    forward(5, 1, copy=U6)
    batch_start(U6)
    forward(6, 0)
    batch_start(7)

    for q in range(3):
        st[RELAX, q, MID_P, MID_R] = g[q + 1]

    @pl.when(y < 3)
    def _():
        hop_copy().wait_recv()

    st[RELAX, 3, MID_P, MID_R] = gn[...]
    g0[pl.ds(0, PLANES), MID_R] = g[0]
    batch_start(RELAX)
    coefficients(3)
    batch_wait(U2)
    coefficients(2, U2)
    coefficients(5)
    coefficients(4)
    batch_wait(U6)
    coefficients(6, U6)
    batch_wait(7)
    coefficients(7)
    batch_wait(RELAX)

    for n in range(2):
        for i in range(4):
            adjoint(RELAX + 4 * n + i, 7 - 4 * n - i, 3 - i)
        batch_start(RELAX + 4 * n + 4)
        batch_wait(RELAX + 4 * n + 4)

    def err_field(i):
        return (
            lambda lo, m: err.at[i, pl.ds(lo, m)],
            lambda k, lo, m: eys.at[k, 0, pl.ds(lo, m)],
            lambda k, lo, m: eyh.at[k, 0, pl.ds(lo, m)],
        )

    cross = (err_field(4), err_field(0), lambda side: ce_send.at[side], lambda side: ce_recv.at[side])

    def block_copy():
        return pltpu.make_async_remote_copy(
            src_ref=eo, dst_ref=ei, send_sem=ce_send.at[8], recv_sem=ce_recv.at[8],
            device_id=dev(px, (y + 3) % 4, z), device_id_type=MESH,
        )

    def give(q, i, start):
        src = cor.at[q, pl.ds(4 * i, 4)]
        z_, px_ = 2 * (2 * c + i) + q // 2, x * 2 + q % 2
        if start:
            push(src, out.at[0, pl.ds(0, 4), pl.ds(pl.multiple_of(z * ROWS, ROWS), ROWS)], co_send.at[q, i], co_recv.at[z], px_, y, z_)
        else:
            push_done(src, co_send.at[q, i], px_, y, z_)

    @pl.when(y < 3)
    def _():
        halo_landed(cross[1], cross[3])
        block_copy().wait_recv()
        err[0, MID_P, MID_R] = ei[...]
        unpack(err.at[0], eyh.at[pl.ds(0, 2), 0])

    array, entry = PLACE[0]
    for i in range(4):
        q = 3 - i
        for lo, hi in chunks(3 - i):
            n = hi - lo
            vv = err[i, pl.ds(lo - 1, n + 2)]
            before = st[RELAX, q - 1, pl.ds(lo, n)] if q else g0[pl.ds(lo - H, n)]
            res = st[RELAX + 8, q, pl.ds(lo, n)] - before
            new = (vv[1:-1] + float(LEVELS) * change(vv, array, entry, q, lo, n)) + res
            err[i + 1, pl.ds(lo, n)] = jnp.where(bb[pl.ds(lo, n)] > 0.0, new, 0.0)

    @pl.when(y > 0)
    def _():
        eo[...] = err[4, MID_P, MID_R]
        pack(err.at[4], eys.at[pl.ds(0, 2), 0])
        block_copy().start()
        halo_start(*cross, y - 1)

    for q in range(4):
        st[FINAL, q, MID_P] = st[RELAX, q, MID_P] + err[3 - q, MID_P]
    batch_start(FINAL)
    for q in range(4):
        cor[q] = g[q] + err[4 - q, MID_P, MID_R]
        for k in range(2):
            give(q, k, True)

    total[...] = jnp.zeros(total.shape, F32)

    def spread(idx, j):
        def one(q):
            for lo, hi in chunks(0):
                n = hi - lo
                first, last = edges(n)
                uu = st[field_of(j), q, pl.ds(lo - 1, n + 2)]
                vv = st[idx, q, pl.ds(lo - 1, n + 2)]
                u, v = uu[1:-1], vv[1:-1]
                f = (uu[1:] - uu[:-1]) * (vv[1:] - vv[:-1])
                acc = f[1:] + f[:-1]
                f = (up(u) - u) * (up(v) - v)
                acc = acc + (f + down(f))
                f = (jnp.where(last, 0.0, right(u)) - u) * (jnp.where(last, 0.0, right(v)) - v)
                acc = acc + (f + jnp.where(first, u * v, left(f)))
                at = pl.ds(lo - H, n)
                total[at] = total[at] - ((0.5 * RATE) * (1.0 + SLOPE * u)) * acc

        per_q(one)

    batch_wait(FINAL)
    batch_sent(RELAX + 4)
    batch_sent(RELAX + 8)
    for i in range(4):
        adjoint(FINAL + i, 7 - i, 3 - i)
    batch_start(FINAL + 4)
    for i in range(4):
        spread(FINAL + i, 7 - i)
    batch_wait(FINAL + 4)
    for i in range(4, 8):
        if i < 7:
            adjoint(FINAL + i, 7 - i, 7 - i)
        spread(FINAL + i, 7 - i)

    turned[...] = jnp.transpose(total[:, pl.ds(H, ROWS)].reshape(PLANES * ROWS, LANES))

    def sum_copy(dy):
        y_ = (y + dy) % 4
        src = turned.at[pl.ds(pl.multiple_of(y_ * 32, 32), 32)]
        return pltpu.make_async_remote_copy(
            src_ref=src, dst_ref=sr.at[dy - 1], send_sem=r1_send.at[dy - 1], recv_sem=r1_recv.at[dy - 1],
            device_id=dev(px, y_, z), device_id_type=MESH,
        )

    for dy in range(1, 4):
        sum_copy(dy).start()
    part = turned[pl.ds(pl.multiple_of(y * 32, 32), 32)]
    for dy in range(1, 4):
        sum_copy(dy).wait_recv()
        part = part + sr[dy - 1]
    s2[0] = part
    s2[1] = pltpu.roll(part, 64, 1)

    def share(n, start):
        i, q = n // 4, n % 4
        src = s2.at[i, pl.ds(8 * q, 8)]
        z_, px_ = 2 * (2 * c + i) + q // 2, x * 2 + q % 2
        if start:
            push(src, sf.at[z], r2_send.at[n], r2_recv.at[z], px_, y, z_)
        else:
            push_done(src, r2_send.at[n], px_, y, z_)

    for n in range(8):
        share(n, True)
    for i in range(8):
        arrived(sf.at[i], r2_recv.at[i])
    sens_out[...] = sf[...]

    for n in range(8):
        share(n, False)
    for dy in range(1, 4):
        sum_copy(dy).wait_send()
    for q in range(4):
        for i in range(2):
            give(q, i, False)
    for i in range(8):
        arrived(out.at[0, pl.ds(0, 4), pl.ds(i * ROWS, ROWS)], co_recv.at[i])

    @pl.when(y > 0)
    def _():
        hop_copy().wait_send()
        block_copy().wait_send()
        halo_sent(*cross, y - 1)

    for idx in EXCHANGED:
        if idx not in (RELAX + 4, RELAX + 8):
            batch_sent(idx)
    for n in range(2):
        field, ssem, rsem = static_field(n)
        halo_sent(field, field, ssem, rsem, y, range(2, 8))

    for i in range(2):
        z_ = 2 * mine + i
        push_done(cut(base_src, z_), bs_send.at[i], to_px, y, z_)
        push_done(cut(weight, z_), wt_send.at[i], to_px, y, z_)

    def drain(i, carry):
        z_ = (z + i) % 8
        push_done(cut(ck.at[0], z_), ck_send.at[i], to_px, y, z_)
        push_done(cut(guess.at[0], z_), gu_send.at[i], to_px, y, z_)
        return carry

    lax.fori_loop(0, 8, drain, 0)


def on_device(checkpoints, guess, materials, table, weight):
    dma = pltpu.SemaphoreType.DMA
    vmem = lambda *shape: pltpu.VMEM(shape, F32)
    block = (PLANES, ROWS, LANES)
    corrected, shares = pl.pallas_call(
        kernel,
        out_shape=(
            jax.ShapeDtypeStruct(guess.shape, F32),
            jax.ShapeDtypeStruct((8, 8, LANES), F32),
        ),
        in_specs=[
            pl.BlockSpec(memory_space=pl.ANY),
            pl.BlockSpec(memory_space=pl.ANY),
            pl.BlockSpec(memory_space=pltpu.VMEM),
            pl.BlockSpec(memory_space=pltpu.SMEM),
            pl.BlockSpec(memory_space=pl.ANY),
        ],
        out_specs=(
            pl.BlockSpec(memory_space=pl.ANY),
            pl.BlockSpec(memory_space=pltpu.VMEM),
        ),
        scratch_shapes=[
            vmem(19, Q, PADP, PADR, LANES),
            vmem(len(EXCHANGED), 2, Q, 64, LANES),
            vmem(len(EXCHANGED), 2, Q, 32, LANES),
            vmem(2, Q, 7, 14, PADR, LANES),
            vmem(2, Q, 7, 12, PADR, LANES),
            vmem(2, Q, 7, 10, PADR, LANES),
            vmem(2, Q, 7, 14, PADR, LANES),
            vmem(4, 128, LANES),
            vmem(Q, *block),
            vmem(*block),
            vmem(*block),
            vmem(PADP, PADR, LANES),
            vmem(PADP, PADR, LANES),
            vmem(2, 2, 1, 64, LANES),
            vmem(2, 2, 1, 32, LANES),
            vmem(Q, *block),
            vmem(*block),
            vmem(PLANES, PADR, LANES),
            vmem(Q, *block),
            vmem(5, PADP, PADR, LANES),
            vmem(*block),
            vmem(*block),
            vmem(2, 1, 64, LANES),
            vmem(2, 1, 32, LANES),
            vmem(PLANES, PADR, LANES),
            vmem(LANES, LANES),
            vmem(3, 32, LANES),
            vmem(2, 32, LANES),
            vmem(8, 8, LANES),
            dma((8,)), dma((8,)), dma((8,)), dma((8,)),
            dma((2,)), dma((2,)), dma((2,)), dma((2,)),
            dma((2, 8)), dma((2, 8)),
            dma((len(EXCHANGED), 8)), dma((len(EXCHANGED), 8)),
            dma, dma,
            dma((9,)), dma((9,)),
            dma((4, 2)), dma((8,)),
            dma((3,)), dma((3,)), dma((8,)), dma((8,)),
        ],
        compiler_params=pltpu.CompilerParams(
            collective_id=0, has_side_effects=True, vmem_limit_bytes=60 * 1024 * 1024
        ),
    )(checkpoints, guess, materials, table, weight)
    parts = shares[:, :, :64].reshape(8, 8, 4, 16)
    sensitivity = jnp.transpose(parts, (2, 0, 3, 1)).reshape(4, 128, 8)
    return corrected, sensitivity


def solution(mesh):
    in_specs = (
        P("tm", "space", None, None),
        P("tm", "space", None, None),
        P("space", None, None),
        P(),
        P("space", None, None),
    )
    out_specs = (P("tm", "space", None, None), P("space", None, "tm"))
    return jax.shard_map(
        on_device, mesh=mesh, in_specs=in_specs, out_specs=out_specs, check_vma=False
    )
```

```python
import functools

import jax
import jax.numpy as jnp
from jax import lax
from jax.experimental import pallas as pl
from jax.experimental.pallas import tpu as pltpu
from jax.sharding import PartitionSpec as P

MESH = pl.DeviceIdType.MESH
F32 = jnp.float32

RATE = 0.006
SLOPE = 0.5
LEVELS = 8
Q, PLANES, ROWS, LANES, H = 4, 8, 16, 128, 4
PADP, PADR = PLANES + 2 * H, ROWS + 2 * H
MID_P, MID_R = pl.ds(H, PLANES), pl.ds(0, ROWS)
SIDES = [(-1, 0), (1, 0), (0, -1), (0, 1), (-1, -1), (1, -1), (-1, 1), (1, 1)]
OPPOSITE = [SIDES.index((-dx, -dz)) for dx, dz in SIDES]
RELAX, FINAL, U2, U6 = 8, 9, 17, 18
EXCHANGED = [0, 3, 7, U2, U6, RELAX, RELAX + 4, RELAX + 8, FINAL, FINAL + 4]
WIDTH = [3, 1, 2, 3, 0, 1, 2, 3]
PLACE = [(3, 1), (2, 1), (1, 1), (0, 1), (3, 0), (2, 0), (1, 0), (0, 0)]
COEF_W = [3, 2, 1, 3]
CORNER = [(1, 3, 0), (2, 2, 3), (3, 1, 5)]


def rows_of(width):
    return PADR if width else ROWS


def chunks(width):
    lo, hi = H - width, H + PLANES + width
    parts = -(-(hi - lo) // 5)
    edges = [lo + (hi - lo) * n // parts for n in range(parts + 1)]
    return list(zip(edges[:-1], edges[1:]))


def kernel(
    ck, guess, mats, table, weight,
    out, sens_out,
    st, yh, ys, zh_, zs_, c0, c1, c2, c3, base_src, bb, wt, bwh, bws, bzh, bzs, g, cor, err, eyh, eys, ezh, ezs,
    total, turned, sr, s2, sf,
    ck_send, ck_recv, gu_send, gu_recv, bs_send, bs_recv, wt_send, wt_recv,
    bx_send, bx_recv, ex_send, ex_recv, hop_send, hop_recv,
    ce_send, ce_recv, co_send, co_recv, r1_send, r1_recv, r2_send, r2_recv,
):
    coef = [c0, c1, c2, c3]
    t, s = lax.axis_index("tm"), lax.axis_index("space")
    y, zl, c = t // 4, (t // 2) % 2, t % 2
    x, zh = s // 4, s % 4
    z = zh * 2 + zl
    px = x * 2 + c
    mine = zl * 2 + c
    half = zh % 2

    def dev(px_, y_, z_):
        return {"tm": y_ * 4 + (z_ % 2) * 2 + px_ % 2, "space": (px_ // 2) * 4 + z_ // 2}

    def there(dx, dz):
        ok = jnp.bool_(True)
        if dx:
            ok = px > 0 if dx < 0 else px < 7
        if dz:
            ok_z = z > 0 if dz < 0 else z < 7
            ok = jnp.logical_and(ok, ok_z) if dx else ok_z
        return ok

    near = [(there(dx, dz), px + dx, z + dz) for dx, dz in SIDES]

    barrier = pltpu.get_barrier_semaphore()

    def greet(px_, y_, z_):
        pl.semaphore_signal(barrier, inc=1, device_id=dev(px_, y_, z_), device_id_type=MESH)

    def ring(i, carry):
        z_, px_ = i // 2, x * 2 + i % 2

        @pl.when(jnp.logical_or(z_ != z, px_ != px))
        def _():
            greet(px_, y, z_)

        return carry

    lax.fori_loop(0, 16, ring, 0)
    count = jnp.int32(15)
    far_ok = jnp.where(c == 0, px > 0, px < 7)
    far = jnp.where(c == 0, px - 1, px + 1)
    for dz in (-1, 0, 1):
        ok = jnp.logical_and(far_ok, there(0, dz)) if dz else far_ok

        @pl.when(ok)
        def _(dz=dz):
            greet(far, y, z + dz)

        count = count + ok.astype(jnp.int32)

    for dy in range(1, 4):
        greet(px, (y + dy) % 4, z)
    count = count + 3

    @pl.when(y > 0)
    def _():
        for z_ in range(8):
            greet(x * 2 + zh // 2, 0, z_)

    count = count + jnp.where(y == 0, 24, 0)
    for dy in (-1, 1):
        y_ok = jnp.logical_and(y + dy >= 0, y + dy < 4)
        for ok, px_, z_ in near:
            both = jnp.logical_and(ok, y_ok)

            @pl.when(both)
            def _(px_=px_, z_=z_, dy=dy):
                greet(px_, y + dy, z_)

            count = count + both.astype(jnp.int32)

    def lookup(p, carry):
        ids = mats[p]
        val = jnp.zeros(ids.shape, F32)
        for number in range(8):
            val = val + jnp.where(ids == number, table[number], 0.0)
        base_src[p] = val
        return carry

    lax.fori_loop(0, 4, lookup, 0)

    def clear_corners(axis, sign):
        for n in range(4):
            if SIDES[4 + n][axis] == sign:
                tile = jnp.zeros((8, LANES), F32)
                bzh[0, n, 0] = tile
                bzh[1, n, 0] = tile
                ezh[n, 0] = tile

                def clear(q, carry):
                    for e in range(len(EXCHANGED)):
                        zh_[e, n, q] = tile
                    return carry

                lax.fori_loop(0, Q, clear, 0)

    for side, lo in ((0, 0), (1, H + PLANES)):

        @pl.when(jnp.logical_not(near[side][0]))
        def _(side=side, lo=lo):
            slab = jnp.zeros((H, PADR, LANES), F32)
            for ref in (bb, wt, err.at[0]):
                ref[pl.ds(lo, H)] = slab

            def clear(q, carry):
                for idx in EXCHANGED:
                    st[idx, q, pl.ds(lo, H)] = slab
                return carry

            lax.fori_loop(0, Q, clear, 0)
            clear_corners(0, SIDES[side][0])

    for side, k in ((2, 0), (3, 1)):

        @pl.when(jnp.logical_not(near[side][0]))
        def _(side=side, k=k):
            edge = jnp.zeros((32, LANES), F32)
            for n in range(2):
                bwh[n, k, 0] = edge
            eyh[k, 0] = edge

            def clear(q, carry):
                for n in range(len(EXCHANGED)):
                    yh[n, k, q] = edge
                return carry

            lax.fori_loop(0, Q, clear, 0)
            clear_corners(1, SIDES[side][1])

    @pl.when(y == 3)
    def _():
        err[0] = jnp.zeros((PADP, PADR, LANES), F32)
        st[RELAX, 3, MID_P, MID_R] = jnp.zeros((PLANES, ROWS, LANES), F32)

    pl.semaphore_wait(barrier, count)

    def push(src, dst, ssem, rsem, px_, y_, z_):
        here = jnp.logical_and(jnp.logical_and(px_ == px, z_ == z), y_ == y)

        @pl.when(here)
        def _():
            pltpu.make_async_copy(src, dst, rsem).start()

        @pl.when(jnp.logical_not(here))
        def _():
            pltpu.make_async_remote_copy(
                src_ref=src, dst_ref=dst, send_sem=ssem, recv_sem=rsem,
                device_id=dev(px_, y_, z_), device_id_type=MESH,
            ).start()

    def push_done(src, ssem, px_, y_, z_):
        here = jnp.logical_and(jnp.logical_and(px_ == px, z_ == z), y_ == y)

        @pl.when(jnp.logical_not(here))
        def _():
            pltpu.make_async_copy(src, src, ssem).wait()

    def arrived(dst, rsem):
        pltpu.make_async_copy(dst, dst, rsem).wait()

    to_px = x * 2 + zh // 2
    slot = half * 4 + mine

    def cut(ref, z_):
        return ref.at[pl.ds(0, 4), pl.ds(pl.multiple_of(z_ * ROWS, ROWS), ROWS)]

    def send_ck(i, carry):
        z_ = (z + i) % 8
        push(cut(ck.at[0], z_), st.at[0, mine, pl.ds(H + 4 * half, 4), MID_R], ck_send.at[i], ck_recv.at[slot], to_px, y, z_)
        return carry

    def send_guess(i, carry):
        z_ = (z + i) % 8
        push(cut(guess.at[0], z_), g.at[mine, pl.ds(4 * half, 4)], gu_send.at[i], gu_recv.at[slot], to_px, y, z_)
        return carry

    for i in range(2):
        z_ = 2 * mine + i
        push(cut(base_src, z_), bb.at[pl.ds(H + 4 * half, 4), MID_R], bs_send.at[i], bs_recv.at[half], to_px, y, z_)
    lax.fori_loop(0, 8, send_ck, 0)
    for i in range(2):
        z_ = 2 * mine + i
        push(cut(weight, z_), wt.at[pl.ds(H + 4 * half, 4), MID_R], wt_send.at[i], wt_recv.at[half], to_px, y, z_)

    def outgoing(field, side):
        planes, rows_out, corner_out, _, _ = field
        dx, dz = SIDES[side]
        if dz == 0:
            return planes(H if dx < 0 else PLANES, H)
        return corner_out(side - 4) if dx else rows_out(0 if dz < 0 else 1)

    def landing(field, side):
        planes, _, _, rows_in, corner_in = field
        dx, dz = SIDES[side]
        if dz == 0:
            return planes(0 if dx < 0 else H + PLANES, H)
        return corner_in(side - 4) if dx else rows_in(0 if dz < 0 else 1)

    def halo_copy(field, to, side, ssem, rsem, y_):
        _, px_, z_ = near[side]
        back = OPPOSITE[side]
        return pltpu.make_async_remote_copy(
            src_ref=outgoing(field, side), dst_ref=landing(to, back), send_sem=ssem(side), recv_sem=rsem(back),
            device_id=dev(px_, y_, z_), device_id_type=MESH,
        )

    def halo_start(field, to, ssem, rsem, y_):
        for side in (4, 5, 6, 7, 2, 3, 0, 1):

            @pl.when(near[side][0])
            def _(side=side):
                halo_copy(field, to, side, ssem, rsem, y_).start()

    def halo_sent(field, to, ssem, rsem, y_, sides=range(8)):
        for side in sides:

            @pl.when(near[side][0])
            def _(side=side):
                halo_copy(field, to, side, ssem, rsem, y_).wait_send()

    def halo_landed(field, rsem):
        for side in range(8):

            @pl.when(near[side][0])
            def _(side=side):
                arrived(landing(field, side), rsem(side))

    def pack(block, rows_out, corner_out):
        for p in range(PLANES):
            for k, row in ((0, 0), (1, ROWS - H)):
                rows_out[0][rows_out[1](k, pl.ds(4 * p, 4))] = block[0][block[1](H + p, pl.ds(row, 4))]
        for n in range(4):
            dx, dz = SIDES[4 + n]
            for d, m, at in CORNER:
                plane = H + d - 1 if dx < 0 else H + PLANES - d
                row = 0 if dz < 0 else ROWS - m
                corner_out[0][corner_out[1](n, pl.ds(at, m))] = block[0][block[1](plane, pl.ds(row, m))]

    def unpack(block, rows_in, corner_in):
        for p in range(PLANES):
            for k, row in ((0, PADR - H), (1, ROWS)):
                block[0][block[1](H + p, pl.ds(row, 4))] = rows_in[0][rows_in[1](k, pl.ds(4 * p, 4))]
        for n in range(4):
            dx, dz = SIDES[4 + n]
            for d, m, at in CORNER:
                plane = H - d if dx < 0 else H + PLANES - 1 + d
                row = PADR - m if dz < 0 else ROWS
                block[0][block[1](plane, pl.ds(row, m))] = corner_in[0][corner_in[1](n, pl.ds(at, m))]

    def batch(idx):
        n = EXCHANGED.index(idx)
        all_q = pl.ds(0, Q)
        field = (
            lambda lo, m: st.at[idx, all_q, pl.ds(lo, m), MID_R],
            lambda k: ys.at[n, k],
            lambda k: zs_.at[n, k],
            lambda k: yh.at[n, k],
            lambda k: zh_.at[n, k],
        )
        return n, field, lambda side: ex_send.at[n, side], lambda side: ex_recv.at[n, side]

    def per_q(one):
        def body(q, carry):
            one(q)
            return carry

        lax.fori_loop(0, Q, body, 0)

    def batch_start(idx):
        n, field, ssem, rsem = batch(idx)
        at = lambda q: (lambda k, rows: (n, k, q, rows))
        per_q(lambda q: pack((st, lambda p, rows: (idx, q, p, rows)), (ys, at(q)), (zs_, at(q))))
        halo_start(field, field, ssem, rsem, y)

    def batch_wait(idx):
        n, field, ssem, rsem = batch(idx)
        halo_landed(field, rsem)
        at = lambda q: (lambda k, rows: (n, k, q, rows))
        per_q(lambda q: unpack((st, lambda p, rows: (idx, q, p, rows)), (yh, at(q)), (zh_, at(q))))

    def batch_sent(idx):
        n, field, ssem, rsem = batch(idx)
        halo_sent(field, field, ssem, rsem, y)

    def static_field(n):
        ref = bb if n == 0 else wt
        field = (
            lambda lo, m: ref.at[pl.ds(lo, m), MID_R],
            lambda k: bws.at[n, k, 0],
            lambda k: bzs.at[n, k, 0],
            lambda k: bwh.at[n, k, 0],
            lambda k: bzh.at[n, k, 0],
        )
        return field, lambda side: bx_send.at[n, side], lambda side: bx_recv.at[n, side]

    def static_start(n):
        ref, sem = (bb, bs_recv) if n == 0 else (wt, wt_recv)
        for i in range(2):
            arrived(ref.at[pl.ds(H + 4 * i, 4), MID_R], sem.at[i])
        at = lambda k, rows: (n, k, 0, rows)
        pack((ref, lambda p, rows: (p, rows)), (bws, at), (bzs, at))
        field, ssem, rsem = static_field(n)
        halo_start(field, field, ssem, rsem, y)

    def static_wait(n):
        field, ssem, rsem = static_field(n)
        halo_landed(field, rsem)
        at = lambda k, rows: (n, k, 0, rows)
        unpack((bb if n == 0 else wt, lambda p, rows: (p, rows)), (bwh, at), (bzh, at))

    static_start(0)
    for i in range(8):
        arrived(st.at[0, i % 4, pl.ds(H + 4 * (i // 4), 4), MID_R], ck_recv.at[i])
    batch_start(0)
    static_start(1)
    static_wait(0)
    batch_wait(0)
    lax.fori_loop(0, 4, send_guess, 0)

    def edges(n, rows):
        lane = lax.broadcasted_iota(jnp.int32, (n, rows, LANES), 2)
        return lane == 0, lane == LANES - 1

    def up(a):
        return pltpu.roll(a, PADR - 1, 1)

    def down(a):
        return pltpu.roll(a, 1, 1)

    def right(a):
        return pltpu.roll(a, LANES - 1, 2)

    def left(a):
        return pltpu.roll(a, 1, 2)

    def forward(j, width, copy=None):
        rows = rows_of(width)

        def one(q):
            for lo, hi in chunks(width):
                n = hi - lo
                first, last = edges(n, rows)
                uu = st[j, q, pl.ds(lo - 1, n + 2)]
                kk = bb[pl.ds(lo - 1, n + 2)] * (1.0 + SLOPE * uu)
                u, k = uu[1:-1], kk[1:-1]
                f = (k + up(k)) * (up(u) - u)
                flow = (f - down(f))[:, :rows]
                uu, kk, u, k = uu[:, :rows], kk[:, :rows], u[:, :rows], k[:, :rows]
                f = (kk[1:] + kk[:-1]) * (uu[1:] - uu[:-1])
                flow = flow + (f[1:] - f[:-1])
                f = (k + jnp.where(last, 0.0, right(k))) * (jnp.where(last, 0.0, right(u)) - u)
                flow = flow + (f - jnp.where(first, k * u, left(f)))
                new = u + (0.5 * RATE) * flow
                if width:
                    new = jnp.where(bb[pl.ds(lo, n)] > 0.0, new, 0.0)
                st[j + 1, q, pl.ds(lo, n), pl.ds(0, rows)] = new
                if copy is not None:
                    a, z_ = max(lo, H), min(hi, H + PLANES)
                    if a < z_:
                        st[copy, q, pl.ds(a, z_ - a), MID_R] = new[a - lo : z_ - lo, :ROWS]

        per_q(one)

    def coefficients(j, field=None):
        idx = j if field is None else field
        array, entry = PLACE[j]
        ref, off = coef[array], H - COEF_W[array]
        rows = rows_of(WIDTH[j])

        def one(q):
            for lo, hi in chunks(WIDTH[j]):
                n = hi - lo
                first, last = edges(n, rows)
                uu = st[idx, q, pl.ds(lo - 1, n + 2)]
                base = bb[pl.ds(lo - 1, n + 2)]
                kk = (0.5 * RATE) * (base * (1.0 + SLOPE * uu))
                u, k = uu[1:-1], kk[1:-1]
                b = (0.25 * RATE) * base[1:-1, :rows]
                at = lambda i: (entry, q, i, pl.ds(lo - off, n), pl.ds(0, rows))
                a, d = k + up(k), up(u) - u
                less, more = down(a)[:, :rows] + b * down(d)[:, :rows], a[:, :rows] - b * d[:, :rows]
                ref[at(3)] = less
                ref[at(4)] = more
                w_sum = less + more
                uu, kk, u, k = uu[:, :rows], kk[:, :rows], u[:, :rows], k[:, :rows]
                a, d = kk[1:] + kk[:-1], uu[1:] - uu[:-1]
                less, more = a[:-1] + b * d[:-1], a[1:] - b * d[1:]
                ref[at(1)] = less
                ref[at(2)] = more
                w_sum = w_sum + (less + more)
                a, d = k + right(k), right(u) - u
                less, more = left(a) + b * left(d), a - b * d
                ref[at(5)] = jnp.where(first, 0.0, less)
                ref[at(6)] = jnp.where(last, 0.0, more)
                edge = k + b * u
                w_sum = w_sum + (jnp.where(first, edge, less) + jnp.where(last, edge, more))
                ref[at(0)] = w_sum

        per_q(one)

    def change(vv, array, entry, q, lo, n, rows):
        ref, off = coef[array], H - COEF_W[array]
        w = lambda i: ref[entry, q, i, pl.ds(lo - off, n), pl.ds(0, rows)]
        acc = down(vv[1:-1])[:, :rows] * w(3)
        acc = acc + up(vv[1:-1])[:, :rows] * w(4)
        vv = vv[:, :rows]
        v = vv[1:-1]
        acc = acc + (vv[:-2] * w(1) + vv[2:] * w(2))
        acc = acc + left(v) * w(5)
        acc = acc + right(v) * w(6)
        return v, acc - v * w(0)

    def field_of(j):
        return {2: U2, 6: U6}.get(j, j)

    def adjoint(idx, j, width):
        array, entry = PLACE[j]
        rows = rows_of(width)
        some = pl.ds(0, rows)

        def one(q):
            for lo, hi in chunks(width):
                n = hi - lo
                at = pl.ds(lo, n)
                v, more = change(st[idx, q, pl.ds(lo - 1, n + 2)], array, entry, q, lo, n, rows)
                new = (v + more) + wt[at, some] * st[field_of(j), q, at, some]
                if width:
                    new = jnp.where(bb[at] > 0.0, new, 0.0)
                st[idx + 1, q, at, some] = new

        per_q(one)

    def hop_copy():
        return pltpu.make_async_remote_copy(
            src_ref=g.at[0], dst_ref=st.at[RELAX, 3, MID_P, MID_R], send_sem=hop_send, recv_sem=hop_recv,
            device_id=dev(px, (y + 3) % 4, z), device_id_type=MESH,
        )

    forward(0, 2)
    forward(1, 1, copy=U2)
    forward(2, 0)
    batch_start(3)

    def rest(i, carry):
        return send_guess(i + 4, carry)

    lax.fori_loop(0, 4, rest, 0)
    static_wait(1)
    coefficients(0)
    coefficients(1)
    batch_wait(3)
    batch_start(U2)
    forward(3, 3)
    for i in range(8):
        arrived(g.at[i % 4, pl.ds(4 * (i // 4), 4)], gu_recv.at[i])

    @pl.when(y > 0)
    def _():
        hop_copy().start()

    for q in range(3):
        st[RELAX, q, MID_P, MID_R] = g[q + 1]
    forward(4, 2)
    forward(5, 1, copy=U6)
    forward(6, 0)
    batch_start(7)

    @pl.when(y < 3)
    def _():
        hop_copy().wait_recv()

    batch_start(RELAX)
    batch_start(U6)
    coefficients(3)
    coefficients(5)
    coefficients(4)
    batch_wait(U2)
    coefficients(2, U2)
    batch_wait(7)
    coefficients(7)
    batch_wait(U6)
    coefficients(6, U6)
    batch_wait(RELAX)

    for n in range(2):
        for i in range(4):
            adjoint(RELAX + 4 * n + i, 7 - 4 * n - i, 3 - i)
        batch_start(RELAX + 4 * n + 4)
        batch_wait(RELAX + 4 * n + 4)

    def err_field(i):
        return (
            lambda lo, m: err.at[i, pl.ds(lo, m), MID_R],
            lambda k: eys.at[k, 0],
            lambda k: ezs.at[k, 0],
            lambda k: eyh.at[k, 0],
            lambda k: ezh.at[k, 0],
        )

    cross = (err_field(4), err_field(0), lambda side: ce_send.at[side], lambda side: ce_recv.at[side])

    def block_copy():
        return pltpu.make_async_remote_copy(
            src_ref=err.at[4, MID_P, MID_R], dst_ref=err.at[0, MID_P, MID_R], send_sem=ce_send.at[8], recv_sem=ce_recv.at[8],
            device_id=dev(px, (y + 3) % 4, z), device_id_type=MESH,
        )

    def packed(k, rows):
        return (k, 0, rows)

    def give(q, i, start):
        src = cor.at[q, pl.ds(4 * i, 4)]
        z_, px_ = 2 * (2 * c + i) + q // 2, x * 2 + q % 2
        if start:
            push(src, out.at[0, pl.ds(0, 4), pl.ds(pl.multiple_of(z * ROWS, ROWS), ROWS)], co_send.at[q, i], co_recv.at[z], px_, y, z_)
        else:
            push_done(src, co_send.at[q, i], px_, y, z_)

    @pl.when(y < 3)
    def _():
        halo_landed(cross[1], cross[3])
        block_copy().wait_recv()
        unpack((err, lambda p, rows: (0, p, rows)), (eyh, packed), (ezh, packed))

    array, entry = PLACE[0]
    for i in range(4):
        q = 3 - i
        rows = rows_of(3 - i)
        some = pl.ds(0, rows)
        for lo, hi in chunks(3 - i):
            n = hi - lo
            at = pl.ds(lo, n)
            e, more = change(err[i, pl.ds(lo - 1, n + 2)], array, entry, q, lo, n, rows)
            before = st[RELAX, q - 1, at, some] if q else g[0, pl.ds(lo - H, n)]
            res = st[RELAX + 8, q, at, some] - before
            new = (e + float(LEVELS) * more) + res
            if i < 3:
                new = jnp.where(bb[at] > 0.0, new, 0.0)
            err[i + 1, at, some] = new

    @pl.when(y > 0)
    def _():
        block_copy().start()
        pack((err, lambda p, rows: (4, p, rows)), (eys, packed), (ezs, packed))
        halo_start(*cross, y - 1)

    for q in range(4):
        st[FINAL, q, MID_P, MID_R] = st[RELAX, q, MID_P, MID_R] + err[3 - q, MID_P, MID_R]
    batch_start(FINAL)
    for q in range(4):
        cor[q] = g[q] + err[4 - q, MID_P, MID_R]

    total[...] = jnp.zeros(total.shape, F32)

    def spread(idx, j):
        def one(q):
            for lo, hi in chunks(0):
                n = hi - lo
                first, last = edges(n, ROWS)
                uu = st[field_of(j), q, pl.ds(lo - 1, n + 2)]
                vv = st[idx, q, pl.ds(lo - 1, n + 2)]
                u, v = uu[1:-1], vv[1:-1]
                f = (up(u) - u) * (up(v) - v)
                acc = (f + down(f))[:, :ROWS]
                uu, vv, u, v = uu[:, :ROWS], vv[:, :ROWS], u[:, :ROWS], v[:, :ROWS]
                f = (uu[1:] - uu[:-1]) * (vv[1:] - vv[:-1])
                acc = acc + (f[1:] + f[:-1])
                f = (jnp.where(last, 0.0, right(u)) - u) * (jnp.where(last, 0.0, right(v)) - v)
                acc = acc + (f + jnp.where(first, u * v, left(f)))
                at = pl.ds(lo - H, n)
                total[at] = total[at] - ((0.5 * RATE) * (1.0 + SLOPE * u)) * acc

        per_q(one)

    batch_wait(FINAL)
    batch_sent(RELAX + 4)
    batch_sent(RELAX + 8)
    for i in range(4):
        adjoint(FINAL + i, 7 - i, 3 - i)
    batch_start(FINAL + 4)
    for i in range(4):
        spread(FINAL + i, 7 - i)
    batch_wait(FINAL + 4)
    for q in range(4):
        for k in range(2):
            give(q, k, True)
    for i in range(4, 8):
        if i < 7:
            adjoint(FINAL + i, 7 - i, 7 - i)
        spread(FINAL + i, 7 - i)

    turned[...] = jnp.transpose(total[...].reshape(PLANES * ROWS, LANES))

    def sum_copy():
        return pltpu.make_async_remote_copy(
            src_ref=turned, dst_ref=sr.at[jnp.maximum(y - 1, 0)], send_sem=r1_send, recv_sem=r1_recv.at[jnp.maximum(y - 1, 0)],
            device_id=dev(px, 0, z), device_id_type=MESH,
        )

    def share(n, start):
        y_, i, q = n // 8, (n // 4) % 2, n % 4
        src = s2.at[i, pl.ds(pl.multiple_of(32 * y_ + 8 * q, 8), 8)]
        z_, px_ = 2 * (2 * c + i) + q // 2, x * 2 + q % 2
        if start:
            push(src, sf.at[z], r2_send.at[n], r2_recv.at[z], px_, y_, z_)
        else:
            push_done(src, r2_send.at[n], px_, y_, z_)

    def share_start(n, carry):
        share(n, True)
        return carry

    def share_done(n, carry):
        share(n, False)
        return carry

    @pl.when(y > 0)
    def _():
        sum_copy().start()

    @pl.when(y == 0)
    def _():
        part = turned[...]
        for n in range(3):
            arrived(sr.at[n], r1_recv.at[n])
            part = part + sr[n]
        s2[0] = part
        s2[1] = pltpu.roll(part, 64, 1)
        lax.fori_loop(0, 32, share_start, 0)

    for i in range(8):
        arrived(sf.at[i], r2_recv.at[i])
    sens_out[...] = sf[...]

    @pl.when(y > 0)
    def _():
        sum_copy().wait_send()

    @pl.when(y == 0)
    def _():
        lax.fori_loop(0, 32, share_done, 0)

    for q in range(4):
        for i in range(2):
            give(q, i, False)
    for i in range(8):
        arrived(out.at[0, pl.ds(0, 4), pl.ds(i * ROWS, ROWS)], co_recv.at[i])

    @pl.when(y > 0)
    def _():
        hop_copy().wait_send()
        block_copy().wait_send()
        halo_sent(*cross, y - 1)

    for idx in EXCHANGED:
        if idx not in (RELAX + 4, RELAX + 8):
            batch_sent(idx)
    for n in range(2):
        field, ssem, rsem = static_field(n)
        halo_sent(field, field, ssem, rsem, y)

    for i in range(2):
        z_ = 2 * mine + i
        push_done(cut(base_src, z_), bs_send.at[i], to_px, y, z_)
        push_done(cut(weight, z_), wt_send.at[i], to_px, y, z_)

    def drain(i, carry):
        z_ = (z + i) % 8
        push_done(cut(ck.at[0], z_), ck_send.at[i], to_px, y, z_)
        push_done(cut(guess.at[0], z_), gu_send.at[i], to_px, y, z_)
        return carry

    lax.fori_loop(0, 8, drain, 0)


def on_device(checkpoints, guess, materials, table, weight):
    dma = pltpu.SemaphoreType.DMA
    vmem = lambda *shape: pltpu.VMEM(shape, F32)
    block = (PLANES, ROWS, LANES)
    corrected, shares = pl.pallas_call(
        kernel,
        out_shape=(
            jax.ShapeDtypeStruct(guess.shape, F32),
            jax.ShapeDtypeStruct((8, 8, LANES), F32),
        ),
        in_specs=[
            pl.BlockSpec(memory_space=pl.ANY),
            pl.BlockSpec(memory_space=pl.ANY),
            pl.BlockSpec(memory_space=pltpu.VMEM),
            pl.BlockSpec(memory_space=pltpu.SMEM),
            pl.BlockSpec(memory_space=pl.ANY),
        ],
        out_specs=(
            pl.BlockSpec(memory_space=pl.ANY),
            pl.BlockSpec(memory_space=pltpu.VMEM),
        ),
        scratch_shapes=[
            vmem(19, Q, PADP, PADR, LANES),
            vmem(len(EXCHANGED), 2, Q, 32, LANES),
            vmem(len(EXCHANGED), 2, Q, 32, LANES),
            vmem(len(EXCHANGED), 4, Q, 8, LANES),
            vmem(len(EXCHANGED), 4, Q, 8, LANES),
            vmem(2, Q, 7, 14, PADR, LANES),
            vmem(2, Q, 7, 12, PADR, LANES),
            vmem(2, Q, 7, 10, PADR, LANES),
            vmem(2, Q, 7, 14, PADR, LANES),
            vmem(4, 128, LANES),
            vmem(PADP, PADR, LANES),
            vmem(PADP, PADR, LANES),
            vmem(2, 2, 1, 32, LANES),
            vmem(2, 2, 1, 32, LANES),
            vmem(2, 4, 1, 8, LANES),
            vmem(2, 4, 1, 8, LANES),
            vmem(Q, *block),
            vmem(Q, *block),
            vmem(5, PADP, PADR, LANES),
            vmem(2, 1, 32, LANES),
            vmem(2, 1, 32, LANES),
            vmem(4, 1, 8, LANES),
            vmem(4, 1, 8, LANES),
            vmem(*block),
            vmem(LANES, LANES),
            vmem(3, LANES, LANES),
            vmem(2, LANES, LANES),
            vmem(8, 8, LANES),
            dma((8,)), dma((8,)), dma((8,)), dma((8,)),
            dma((2,)), dma((2,)), dma((2,)), dma((2,)),
            dma((2, 8)), dma((2, 8)),
            dma((len(EXCHANGED), 8)), dma((len(EXCHANGED), 8)),
            dma, dma,
            dma((9,)), dma((9,)),
            dma((4, 2)), dma((8,)),
            dma, dma((3,)), dma((32,)), dma((8,)),
        ],
        compiler_params=pltpu.CompilerParams(
            collective_id=0, has_side_effects=True, vmem_limit_bytes=60 * 1024 * 1024
        ),
    )(checkpoints, guess, materials, table, weight)
    parts = shares[:, :, :64].reshape(8, 8, 4, 16)
    sensitivity = jnp.transpose(parts, (2, 0, 3, 1)).reshape(4, 128, 8)
    return corrected, sensitivity


def solution(mesh):
    in_specs = (
        P("tm", "space", None, None),
        P("tm", "space", None, None),
        P("space", None, None),
        P(),
        P("space", None, None),
    )
    out_specs = (P("tm", "space", None, None), P("space", None, "tm"))
    return jax.shard_map(
        on_device, mesh=mesh, in_specs=in_specs, out_specs=out_specs, check_vma=False
    )
```

```python
import functools

import jax
import jax.numpy as jnp
from jax import lax
from jax.experimental import pallas as pl
from jax.experimental.pallas import tpu as pltpu
from jax.sharding import PartitionSpec as P

MESH = pl.DeviceIdType.MESH
F32 = jnp.float32

RATE = 0.006
SLOPE = 0.5
LEVELS = 8
Q, PLANES, ROWS, LANES, H = 4, 8, 16, 128, 4
PADP, PADR = PLANES + 2 * H, ROWS + 2 * H
MID_P, MID_R = pl.ds(H, PLANES), pl.ds(0, ROWS)
SIDES = [(-1, 0), (1, 0), (0, -1), (0, 1), (-1, -1), (1, -1), (-1, 1), (1, 1)]
OPPOSITE = [SIDES.index((-dx, -dz)) for dx, dz in SIDES]
RELAX, FINAL, U2, U6 = 8, 9, 17, 18
EXCHANGED = [0, 3, 7, U2, U6, RELAX, RELAX + 4, RELAX + 8, FINAL, FINAL + 4]
SOME = {RELAX + 8: (1, 3), FINAL: (0, 3)}
WIDTH = [3, 1, 2, 3, 0, 1, 2, 3]
PLACE = [(3, 1), (2, 1), (1, 1), (0, 1), (3, 0), (2, 0), (1, 0), (0, 0)]
COEF_W = [3, 2, 1, 3]
CORNER = [(1, 3, 0), (2, 2, 3), (3, 1, 5)]


def rows_of(width):
    return PADR if width else ROWS


def chunks(width):
    lo, hi = H - width, H + PLANES + width
    parts = -(-(hi - lo) // 5)
    edges = [lo + (hi - lo) * n // parts for n in range(parts + 1)]
    return list(zip(edges[:-1], edges[1:]))


def kernel(
    ck, guess, mats, table, weight,
    out, sens_out,
    st, yh, ys, zh_, zs_, c0, c1, c2, c3, base_src, bb, wt, bwh, bws, bzh, bzs, g, cor, err, eyh, eys, ezh, ezs,
    total, turned, sr, s2, sf, ids_, id_sem,
    ck_send, ck_recv, gu_send, gu_recv, bs_send, bs_recv, wt_send, wt_recv,
    bx_send, bx_recv, ex_send, ex_recv, hop_send, hop_recv,
    ce_send, ce_recv, co_send, co_recv, r1_send, r1_recv, r2_send, r2_recv,
):
    coef = [c0, c1, c2, c3]
    t, s = lax.axis_index("tm"), lax.axis_index("space")
    y, zl, c = t // 4, (t // 2) % 2, t % 2
    x, zh = s // 4, s % 4
    z = zh * 2 + zl
    px = x * 2 + c
    mine = zl * 2 + c
    half = zh % 2

    def dev(px_, y_, z_):
        return {"tm": y_ * 4 + (z_ % 2) * 2 + px_ % 2, "space": (px_ // 2) * 4 + z_ // 2}

    def there(dx, dz):
        ok = jnp.bool_(True)
        if dx:
            ok = px > 0 if dx < 0 else px < 7
        if dz:
            ok_z = z > 0 if dz < 0 else z < 7
            ok = jnp.logical_and(ok, ok_z) if dx else ok_z
        return ok

    near = [(there(dx, dz), px + dx, z + dz) for dx, dz in SIDES]

    barrier = pltpu.get_barrier_semaphore()
    fetch = pltpu.make_async_copy(mats, ids_, id_sem)
    fetch.start()

    def greet(px_, y_, z_):
        pl.semaphore_signal(barrier, inc=1, device_id=dev(px_, y_, z_), device_id_type=MESH)

    def ring(i, carry):
        z_, px_ = i // 2, x * 2 + i % 2

        @pl.when(jnp.logical_or(z_ != z, px_ != px))
        def _():
            greet(px_, y, z_)

        return carry

    lax.fori_loop(0, 16, ring, 0)
    count = jnp.int32(15)
    far_ok = jnp.where(c == 0, px > 0, px < 7)
    far = jnp.where(c == 0, px - 1, px + 1)
    for dz in (-1, 0, 1):
        ok = jnp.logical_and(far_ok, there(0, dz)) if dz else far_ok

        @pl.when(ok)
        def _(dz=dz):
            greet(far, y, z + dz)

        count = count + ok.astype(jnp.int32)

    for dy in range(1, 4):
        greet(px, (y + dy) % 4, z)
    count = count + 3

    @pl.when(y > 0)
    def _():
        for z_ in range(8):
            greet(x * 2 + zh // 2, 0, z_)

    count = count + jnp.where(y == 0, 24, 0)
    for ok, px_, z_ in near:

        @pl.when(jnp.logical_and(ok, y < 3))
        def _(px_=px_, z_=z_):
            greet(px_, y + 1, z_)

        count = count + jnp.logical_and(ok, y > 0).astype(jnp.int32)

    def lookup(p, carry):
        ids = ids_[p]
        val = jnp.zeros(ids.shape, F32)
        for number in range(8):
            val = val + jnp.where(ids == number, table[number], 0.0)
        base_src[p] = val
        return carry

    fetch.wait()
    lax.fori_loop(0, 4, lookup, 0)

    def clear_corners(axis, sign):
        for n in range(4):
            if SIDES[4 + n][axis] == sign:
                tile = jnp.zeros((8, LANES), F32)
                bzh[0, n, 0] = tile
                bzh[1, n, 0] = tile
                ezh[n, 0] = tile

                def clear(q, carry):
                    for e in range(len(EXCHANGED)):
                        zh_[e, n, q] = tile
                    return carry

                lax.fori_loop(0, Q, clear, 0)

    for side, lo in ((0, 0), (1, H + PLANES)):

        @pl.when(jnp.logical_not(near[side][0]))
        def _(side=side, lo=lo):
            slab = jnp.zeros((H, PADR, LANES), F32)
            for ref in (bb, wt, err.at[0]):
                ref[pl.ds(lo, H)] = slab

            def clear(q, carry):
                for idx in EXCHANGED:
                    st[idx, q, pl.ds(lo, H)] = slab
                return carry

            lax.fori_loop(0, Q, clear, 0)
            clear_corners(0, SIDES[side][0])

    for side, k in ((2, 0), (3, 1)):

        @pl.when(jnp.logical_not(near[side][0]))
        def _(side=side, k=k):
            edge = jnp.zeros((32, LANES), F32)
            for n in range(2):
                bwh[n, k, 0] = edge
            eyh[k, 0] = edge

            def clear(q, carry):
                for n in range(len(EXCHANGED)):
                    yh[n, k, q] = edge
                return carry

            lax.fori_loop(0, Q, clear, 0)
            clear_corners(1, SIDES[side][1])

    @pl.when(y == 3)
    def _():
        err[0] = jnp.zeros((PADP, PADR, LANES), F32)
        st[RELAX, 3, MID_P, MID_R] = jnp.zeros((PLANES, ROWS, LANES), F32)

    pl.semaphore_wait(barrier, count)

    def push(src, dst, ssem, rsem, px_, y_, z_):
        here = jnp.logical_and(jnp.logical_and(px_ == px, z_ == z), y_ == y)

        @pl.when(here)
        def _():
            pltpu.make_async_copy(src, dst, rsem).start()

        @pl.when(jnp.logical_not(here))
        def _():
            pltpu.make_async_remote_copy(
                src_ref=src, dst_ref=dst, send_sem=ssem, recv_sem=rsem,
                device_id=dev(px_, y_, z_), device_id_type=MESH,
            ).start()

    def push_done(src, ssem, px_, y_, z_):
        here = jnp.logical_and(jnp.logical_and(px_ == px, z_ == z), y_ == y)

        @pl.when(jnp.logical_not(here))
        def _():
            pltpu.make_async_copy(src, src, ssem).wait()

    def arrived(dst, rsem):
        pltpu.make_async_copy(dst, dst, rsem).wait()

    to_px = x * 2 + zh // 2
    slot = half * 4 + mine

    def cut(ref, z_):
        return ref.at[pl.ds(0, 4), pl.ds(pl.multiple_of(z_ * ROWS, ROWS), ROWS)]

    def turn(i):
        k = (i + 1) // 2
        return (z + jnp.where(i % 2 == 0, 4 + k, 4 - k)) % 8

    def send_ck(i, carry):
        z_ = turn(i)
        push(cut(ck.at[0], z_), st.at[0, mine, pl.ds(H + 4 * half, 4), MID_R], ck_send.at[i], ck_recv.at[slot], to_px, y, z_)
        return carry

    def send_guess(i, carry):
        z_ = turn(i)
        push(cut(guess.at[0], z_), g.at[mine, pl.ds(4 * half, 4)], gu_send.at[i], gu_recv.at[slot], to_px, y, z_)
        return carry

    for i in range(2):
        z_ = 2 * mine + i
        push(cut(base_src, z_), bb.at[pl.ds(H + 4 * half, 4), MID_R], bs_send.at[i], bs_recv.at[half], to_px, y, z_)
    lax.fori_loop(0, 8, send_ck, 0)

    def outgoing(field, side):
        planes, rows_out, corner_out, _, _ = field
        dx, dz = SIDES[side]
        if dz == 0:
            return planes(H if dx < 0 else PLANES, H)
        return corner_out(side - 4) if dx else rows_out(0 if dz < 0 else 1)

    def landing(field, side):
        planes, _, _, rows_in, corner_in = field
        dx, dz = SIDES[side]
        if dz == 0:
            return planes(0 if dx < 0 else H + PLANES, H)
        return corner_in(side - 4) if dx else rows_in(0 if dz < 0 else 1)

    def halo_copy(field, to, side, ssem, rsem, y_):
        _, px_, z_ = near[side]
        back = OPPOSITE[side]
        return pltpu.make_async_remote_copy(
            src_ref=outgoing(field, side), dst_ref=landing(to, back), send_sem=ssem(side), recv_sem=rsem(back),
            device_id=dev(px_, y_, z_), device_id_type=MESH,
        )

    def halo_start(field, to, ssem, rsem, y_, sides):
        for side in sides:

            @pl.when(near[side][0])
            def _(side=side):
                halo_copy(field, to, side, ssem, rsem, y_).start()

    def halo_sent(field, to, ssem, rsem, y_, sides=range(8)):
        for side in sides:

            @pl.when(near[side][0])
            def _(side=side):
                halo_copy(field, to, side, ssem, rsem, y_).wait_send()

    def halo_landed(field, rsem):
        for side in range(8):

            @pl.when(near[side][0])
            def _(side=side):
                arrived(landing(field, side), rsem(side))

    def pack_corners(block, corner_out):
        for n in range(4):
            dx, dz = SIDES[4 + n]
            for d, m, at in CORNER:
                plane = H + d - 1 if dx < 0 else H + PLANES - d
                row = 0 if dz < 0 else ROWS - m
                corner_out[0][corner_out[1](n, pl.ds(at, m))] = block[0][block[1](plane, pl.ds(row, m))]

    def pack_rows(block, rows_out):
        for p in range(PLANES):
            for k, row in ((0, 0), (1, ROWS - H)):
                rows_out[0][rows_out[1](k, pl.ds(4 * p, 4))] = block[0][block[1](H + p, pl.ds(row, 4))]

    def unpack(block, rows_in, corner_in):
        for p in range(PLANES):
            for k, row in ((0, PADR - H), (1, ROWS)):
                block[0][block[1](H + p, pl.ds(row, 4))] = rows_in[0][rows_in[1](k, pl.ds(4 * p, 4))]
        for n in range(4):
            dx, dz = SIDES[4 + n]
            for d, m, at in CORNER:
                plane = H - d if dx < 0 else H + PLANES - 1 + d
                row = PADR - m if dz < 0 else ROWS
                block[0][block[1](plane, pl.ds(row, m))] = corner_in[0][corner_in[1](n, pl.ds(at, m))]

    def batch(idx):
        n = EXCHANGED.index(idx)
        some = pl.ds(*SOME.get(idx, (0, Q)))
        field = (
            lambda lo, m: st.at[idx, some, pl.ds(lo, m), MID_R],
            lambda k: ys.at[n, k, some],
            lambda k: zs_.at[n, k, some],
            lambda k: yh.at[n, k, some],
            lambda k: zh_.at[n, k, some],
        )
        return n, field, lambda side: ex_send.at[n, side], lambda side: ex_recv.at[n, side]

    def per_q(one, idx=None):
        def body(q, carry):
            one(q)
            return carry

        lo, m = SOME.get(idx, (0, Q))
        lax.fori_loop(lo, lo + m, body, 0)

    def batch_start(idx):
        n, field, ssem, rsem = batch(idx)
        at = lambda q: (lambda k, rows: (n, k, q, rows))
        block = lambda q: (st, lambda p, rows: (idx, q, p, rows))
        per_q(lambda q: pack_corners(block(q), (zs_, at(q))), idx)
        halo_start(field, field, ssem, rsem, y, (4, 5, 6, 7))
        per_q(lambda q: pack_rows(block(q), (ys, at(q))), idx)
        halo_start(field, field, ssem, rsem, y, (2, 3, 0, 1))

    def batch_wait(idx):
        n, field, ssem, rsem = batch(idx)
        halo_landed(field, rsem)
        at = lambda q: (lambda k, rows: (n, k, q, rows))
        per_q(lambda q: unpack((st, lambda p, rows: (idx, q, p, rows)), (yh, at(q)), (zh_, at(q))), idx)

    def batch_sent(idx):
        n, field, ssem, rsem = batch(idx)
        halo_sent(field, field, ssem, rsem, y)

    def static_field(n):
        ref = bb if n == 0 else wt
        field = (
            lambda lo, m: ref.at[pl.ds(lo, m), MID_R],
            lambda k: bws.at[n, k, 0],
            lambda k: bzs.at[n, k, 0],
            lambda k: bwh.at[n, k, 0],
            lambda k: bzh.at[n, k, 0],
        )
        return field, lambda side: bx_send.at[n, side], lambda side: bx_recv.at[n, side]

    def static_start(n):
        ref, sem = (bb, bs_recv) if n == 0 else (wt, wt_recv)
        for i in range(2):
            arrived(ref.at[pl.ds(H + 4 * i, 4), MID_R], sem.at[i])
        at = lambda k, rows: (n, k, 0, rows)
        block = (ref, lambda p, rows: (p, rows))
        pack_corners(block, (bzs, at))
        pack_rows(block, (bws, at))
        field, ssem, rsem = static_field(n)
        halo_start(field, field, ssem, rsem, y, (4, 5, 6, 7, 2, 3, 0, 1))

    def static_wait(n):
        field, ssem, rsem = static_field(n)
        halo_landed(field, rsem)
        at = lambda k, rows: (n, k, 0, rows)
        unpack((bb if n == 0 else wt, lambda p, rows: (p, rows)), (bwh, at), (bzh, at))

    static_start(0)
    for i in range(8):
        arrived(st.at[0, i % 4, pl.ds(H + 4 * (i // 4), 4), MID_R], ck_recv.at[i])
    batch_start(0)
    for i in range(2):
        z_ = 2 * mine + i
        push(cut(weight, z_), wt.at[pl.ds(H + 4 * half, 4), MID_R], wt_send.at[i], wt_recv.at[half], to_px, y, z_)
    static_wait(0)
    batch_wait(0)
    lax.fori_loop(0, 4, send_guess, 0)

    def edges(n, rows):
        lane = lax.broadcasted_iota(jnp.int32, (n, rows, LANES), 2)
        return lane == 0, lane == LANES - 1

    def up(a):
        return pltpu.roll(a, PADR - 1, 1)

    def down(a):
        return pltpu.roll(a, 1, 1)

    def right(a):
        return pltpu.roll(a, LANES - 1, 2)

    def left(a):
        return pltpu.roll(a, 1, 2)

    def forward(j, width, copy=None):
        rows = rows_of(width)

        def one(q):
            for lo, hi in chunks(width):
                n = hi - lo
                first, last = edges(n, rows)
                uu = st[j, q, pl.ds(lo - 1, n + 2)]
                kk = bb[pl.ds(lo - 1, n + 2)] * (1.0 + SLOPE * uu)
                u, k = uu[1:-1], kk[1:-1]
                f = (k + up(k)) * (up(u) - u)
                flow = (f - down(f))[:, :rows]
                uu, kk, u, k = uu[:, :rows], kk[:, :rows], u[:, :rows], k[:, :rows]
                f = (kk[1:] + kk[:-1]) * (uu[1:] - uu[:-1])
                flow = flow + (f[1:] - f[:-1])
                f = (k + jnp.where(last, 0.0, right(k))) * (jnp.where(last, 0.0, right(u)) - u)
                flow = flow + (f - jnp.where(first, k * u, left(f)))
                new = u + (0.5 * RATE) * flow
                if width:
                    new = jnp.where(bb[pl.ds(lo, n)] > 0.0, new, 0.0)
                st[j + 1, q, pl.ds(lo, n), pl.ds(0, rows)] = new
                if copy is not None:
                    a, z_ = max(lo, H), min(hi, H + PLANES)
                    if a < z_:
                        st[copy, q, pl.ds(a, z_ - a), MID_R] = new[a - lo : z_ - lo, :ROWS]

        per_q(one)

    def coefficients(j, field=None):
        idx = j if field is None else field
        array, entry = PLACE[j]
        ref, off = coef[array], H - COEF_W[array]
        rows = rows_of(WIDTH[j])

        def one(q):
            for lo, hi in chunks(WIDTH[j]):
                n = hi - lo
                first, last = edges(n, rows)
                uu = st[idx, q, pl.ds(lo - 1, n + 2)]
                base = bb[pl.ds(lo - 1, n + 2)]
                kk = (0.5 * RATE) * (base * (1.0 + SLOPE * uu))
                u, k = uu[1:-1], kk[1:-1]
                b = (0.25 * RATE) * base[1:-1, :rows]
                at = lambda i: (entry, q, i, pl.ds(lo - off, n), pl.ds(0, rows))
                a, d = k + up(k), up(u) - u
                less, more = down(a)[:, :rows] + b * down(d)[:, :rows], a[:, :rows] - b * d[:, :rows]
                ref[at(3)] = less
                ref[at(4)] = more
                w_sum = less + more
                uu, kk, u, k = uu[:, :rows], kk[:, :rows], u[:, :rows], k[:, :rows]
                a, d = kk[1:] + kk[:-1], uu[1:] - uu[:-1]
                less, more = a[:-1] + b * d[:-1], a[1:] - b * d[1:]
                ref[at(1)] = less
                ref[at(2)] = more
                w_sum = w_sum + (less + more)
                a, d = k + right(k), right(u) - u
                less, more = left(a) + b * left(d), a - b * d
                ref[at(5)] = jnp.where(first, 0.0, less)
                ref[at(6)] = jnp.where(last, 0.0, more)
                edge = k + b * u
                w_sum = w_sum + (jnp.where(first, edge, less) + jnp.where(last, edge, more))
                ref[at(0)] = w_sum

        per_q(one)

    def change(vv, array, entry, q, lo, n, rows):
        ref, off = coef[array], H - COEF_W[array]
        w = lambda i: ref[entry, q, i, pl.ds(lo - off, n), pl.ds(0, rows)]
        acc = down(vv[1:-1])[:, :rows] * w(3)
        acc = acc + up(vv[1:-1])[:, :rows] * w(4)
        vv = vv[:, :rows]
        v = vv[1:-1]
        acc = acc + (vv[:-2] * w(1) + vv[2:] * w(2))
        acc = acc + left(v) * w(5)
        acc = acc + right(v) * w(6)
        return v, acc - v * w(0)

    def field_of(j):
        return {2: U2, 6: U6}.get(j, j)

    def adjoint(idx, j, width):
        array, entry = PLACE[j]
        rows = rows_of(width)
        some = pl.ds(0, rows)

        def one(q):
            for lo, hi in chunks(width):
                n = hi - lo
                at = pl.ds(lo, n)
                v, more = change(st[idx, q, pl.ds(lo - 1, n + 2)], array, entry, q, lo, n, rows)
                new = (v + more) + wt[at, some] * st[field_of(j), q, at, some]
                if width:
                    new = jnp.where(bb[at] > 0.0, new, 0.0)
                st[idx + 1, q, at, some] = new

        per_q(one)

    def hop_copy():
        return pltpu.make_async_remote_copy(
            src_ref=g.at[0], dst_ref=st.at[RELAX, 3, MID_P, MID_R], send_sem=hop_send, recv_sem=hop_recv,
            device_id=dev(px, (y + 3) % 4, z), device_id_type=MESH,
        )

    forward(0, 2)
    forward(1, 1, copy=U2)
    forward(2, 0)
    batch_start(3)
    static_start(1)

    def rest(i, carry):
        return send_guess(i + 4, carry)

    lax.fori_loop(0, 4, rest, 0)
    coefficients(0)
    coefficients(1)
    static_wait(1)
    batch_wait(3)
    batch_start(U2)
    forward(3, 3)
    for i in range(8):
        arrived(g.at[i % 4, pl.ds(4 * (i // 4), 4)], gu_recv.at[i])

    @pl.when(y > 0)
    def _():
        hop_copy().start()

    for q in range(3):
        st[RELAX, q, MID_P, MID_R] = g[q + 1]
    forward(4, 2)
    forward(5, 1, copy=U6)
    forward(6, 0)
    batch_start(7)
    batch_start(U6)

    @pl.when(y < 3)
    def _():
        hop_copy().wait_recv()

    batch_start(RELAX)
    coefficients(5)
    coefficients(4)
    batch_wait(7)
    coefficients(7)
    batch_wait(U6)
    coefficients(6, U6)
    batch_wait(RELAX)
    for i in range(4):
        adjoint(RELAX + i, 7 - i, 3 - i)
    batch_start(RELAX + 4)
    coefficients(3)
    batch_wait(U2)
    coefficients(2, U2)
    batch_wait(RELAX + 4)
    for i in range(4, 8):
        adjoint(RELAX + i, 7 - i, 7 - i)
    batch_start(RELAX + 8)
    batch_wait(RELAX + 8)

    def err_field(i):
        return (
            lambda lo, m: err.at[i, pl.ds(lo, m), MID_R],
            lambda k: eys.at[k, 0],
            lambda k: ezs.at[k, 0],
            lambda k: eyh.at[k, 0],
            lambda k: ezh.at[k, 0],
        )

    cross = (err_field(4), err_field(0), lambda side: ce_send.at[side], lambda side: ce_recv.at[side])

    def block_copy():
        return pltpu.make_async_remote_copy(
            src_ref=err.at[4, MID_P, MID_R], dst_ref=err.at[0, MID_P, MID_R], send_sem=ce_send.at[8], recv_sem=ce_recv.at[8],
            device_id=dev(px, (y + 3) % 4, z), device_id_type=MESH,
        )

    def packed(k, rows):
        return (k, 0, rows)

    def give(q, i, start):
        src = cor.at[q, pl.ds(4 * i, 4)]
        z_, px_ = 2 * (2 * c + i) + q // 2, x * 2 + q % 2
        if start:
            push(src, out.at[0, pl.ds(0, 4), pl.ds(pl.multiple_of(z * ROWS, ROWS), ROWS)], co_send.at[q, i], co_recv.at[z], px_, y, z_)
        else:
            push_done(src, co_send.at[q, i], px_, y, z_)

    @pl.when(y < 3)
    def _():
        halo_landed(cross[1], cross[3])
        block_copy().wait_recv()
        unpack((err, lambda p, rows: (0, p, rows)), (eyh, packed), (ezh, packed))

    def coarse(i):
        q = 3 - i
        array, entry = PLACE[0]
        rows = rows_of(3 - i)
        some = pl.ds(0, rows)
        for lo, hi in chunks(3 - i):
            n = hi - lo
            at = pl.ds(lo, n)
            e, more = change(err[i, pl.ds(lo - 1, n + 2)], array, entry, q, lo, n, rows)
            before = st[RELAX, q - 1, at, some] if q else g[0, pl.ds(lo - H, n)]
            res = st[RELAX + 8, q, at, some] - before
            new = (e + float(LEVELS) * more) + res
            if i < 3:
                new = jnp.where(bb[at] > 0.0, new, 0.0)
            err[i + 1, at, some] = new

    for i in range(3):
        coarse(i)

    @pl.when(y > 0)
    def _():
        coarse(3)
        block = (err, lambda p, rows: (4, p, rows))
        pack_corners(block, (ezs, packed))
        halo_start(*cross, y - 1, (4, 5, 6, 7))
        pack_rows(block, (eys, packed))
        halo_start(*cross, y - 1, (2, 3, 0, 1))
        block_copy().start()

    for q in range(3):
        st[FINAL, q, MID_P, MID_R] = st[RELAX, q, MID_P, MID_R] + err[3 - q, MID_P, MID_R]
    batch_start(FINAL)
    st[FINAL, 3] = st[RELAX, 3] + err[0]

    @pl.when(y == 0)
    def _():
        coarse(3)

    for q in range(4):
        cor[q] = g[q] + err[4 - q, MID_P, MID_R]

    total[...] = jnp.zeros(total.shape, F32)

    def spread(idx, j):
        def one(q):
            for lo, hi in chunks(0):
                n = hi - lo
                first, last = edges(n, ROWS)
                uu = st[field_of(j), q, pl.ds(lo - 1, n + 2)]
                vv = st[idx, q, pl.ds(lo - 1, n + 2)]
                u, v = uu[1:-1], vv[1:-1]
                f = (up(u) - u) * (up(v) - v)
                acc = (f + down(f))[:, :ROWS]
                uu, vv, u, v = uu[:, :ROWS], vv[:, :ROWS], u[:, :ROWS], v[:, :ROWS]
                f = (uu[1:] - uu[:-1]) * (vv[1:] - vv[:-1])
                acc = acc + (f[1:] + f[:-1])
                f = (jnp.where(last, 0.0, right(u)) - u) * (jnp.where(last, 0.0, right(v)) - v)
                acc = acc + (f + jnp.where(first, u * v, left(f)))
                at = pl.ds(lo - H, n)
                total[at] = total[at] - ((0.5 * RATE) * (1.0 + SLOPE * u)) * acc

        per_q(one)

    batch_wait(FINAL)
    batch_sent(RELAX + 4)
    batch_sent(RELAX + 8)
    for i in range(4):
        adjoint(FINAL + i, 7 - i, 3 - i)
    batch_start(FINAL + 4)
    for i in range(4):
        spread(FINAL + i, 7 - i)
    batch_wait(FINAL + 4)
    for q in range(4):
        for k in range(2):
            give(q, k, True)
    for i in range(4, 8):
        if i < 7:
            adjoint(FINAL + i, 7 - i, 7 - i)
        spread(FINAL + i, 7 - i)

    turned[...] = jnp.transpose(total[...].reshape(PLANES * ROWS, LANES))

    def sum_copy():
        return pltpu.make_async_remote_copy(
            src_ref=turned, dst_ref=sr.at[jnp.maximum(y - 1, 0)], send_sem=r1_send, recv_sem=r1_recv.at[jnp.maximum(y - 1, 0)],
            device_id=dev(px, 0, z), device_id_type=MESH,
        )

    def share(n, start):
        y_, i, q = n // 8, (n // 4) % 2, n % 4
        src = s2.at[i, pl.ds(pl.multiple_of(32 * y_ + 8 * q, 8), 8)]
        z_, px_ = 2 * (2 * c + i) + q // 2, x * 2 + q % 2
        if start:
            push(src, sf.at[z], r2_send.at[n], r2_recv.at[z], px_, y_, z_)
        else:
            push_done(src, r2_send.at[n], px_, y_, z_)

    def share_start(n, carry):
        share(n, True)
        return carry

    def share_done(n, carry):
        share(n, False)
        return carry

    @pl.when(y > 0)
    def _():
        sum_copy().start()

    @pl.when(y == 0)
    def _():
        part = turned[...]
        for n in range(3):
            arrived(sr.at[n], r1_recv.at[n])
            part = part + sr[n]
        s2[0] = part
        s2[1] = pltpu.roll(part, 64, 1)
        lax.fori_loop(0, 32, share_start, 0)

    for i in range(8):
        arrived(sf.at[i], r2_recv.at[i])
    sens_out[...] = sf[...]

    @pl.when(y > 0)
    def _():
        sum_copy().wait_send()

    @pl.when(y == 0)
    def _():
        lax.fori_loop(0, 32, share_done, 0)

    for q in range(4):
        for i in range(2):
            give(q, i, False)
    for i in range(8):
        arrived(out.at[0, pl.ds(0, 4), pl.ds(i * ROWS, ROWS)], co_recv.at[i])

    @pl.when(y > 0)
    def _():
        hop_copy().wait_send()
        block_copy().wait_send()
        halo_sent(*cross, y - 1)

    for idx in EXCHANGED:
        if idx not in (RELAX + 4, RELAX + 8):
            batch_sent(idx)
    for n in range(2):
        field, ssem, rsem = static_field(n)
        halo_sent(field, field, ssem, rsem, y)

    for i in range(2):
        z_ = 2 * mine + i
        push_done(cut(base_src, z_), bs_send.at[i], to_px, y, z_)
        push_done(cut(weight, z_), wt_send.at[i], to_px, y, z_)

    def drain(i, carry):
        z_ = turn(i)
        push_done(cut(ck.at[0], z_), ck_send.at[i], to_px, y, z_)
        push_done(cut(guess.at[0], z_), gu_send.at[i], to_px, y, z_)
        return carry

    lax.fori_loop(0, 8, drain, 0)


def on_device(checkpoints, guess, materials, table, weight):
    dma = pltpu.SemaphoreType.DMA
    vmem = lambda *shape: pltpu.VMEM(shape, F32)
    block = (PLANES, ROWS, LANES)
    corrected, shares = pl.pallas_call(
        kernel,
        out_shape=(
            jax.ShapeDtypeStruct(guess.shape, F32),
            jax.ShapeDtypeStruct((8, 8, LANES), F32),
        ),
        in_specs=[
            pl.BlockSpec(memory_space=pl.ANY),
            pl.BlockSpec(memory_space=pl.ANY),
            pl.BlockSpec(memory_space=pl.ANY),
            pl.BlockSpec(memory_space=pltpu.SMEM),
            pl.BlockSpec(memory_space=pl.ANY),
        ],
        out_specs=(
            pl.BlockSpec(memory_space=pl.ANY),
            pl.BlockSpec(memory_space=pltpu.VMEM),
        ),
        scratch_shapes=[
            vmem(19, Q, PADP, PADR, LANES),
            vmem(len(EXCHANGED), 2, Q, 32, LANES),
            vmem(len(EXCHANGED), 2, Q, 32, LANES),
            vmem(len(EXCHANGED), 4, Q, 8, LANES),
            vmem(len(EXCHANGED), 4, Q, 8, LANES),
            vmem(2, Q, 7, 14, PADR, LANES),
            vmem(2, Q, 7, 12, PADR, LANES),
            vmem(2, Q, 7, 10, PADR, LANES),
            vmem(2, Q, 7, 14, PADR, LANES),
            vmem(4, 128, LANES),
            vmem(PADP, PADR, LANES),
            vmem(PADP, PADR, LANES),
            vmem(2, 2, 1, 32, LANES),
            vmem(2, 2, 1, 32, LANES),
            vmem(2, 4, 1, 8, LANES),
            vmem(2, 4, 1, 8, LANES),
            vmem(Q, *block),
            vmem(Q, *block),
            vmem(5, PADP, PADR, LANES),
            vmem(2, 1, 32, LANES),
            vmem(2, 1, 32, LANES),
            vmem(4, 1, 8, LANES),
            vmem(4, 1, 8, LANES),
            vmem(*block),
            vmem(LANES, LANES),
            vmem(3, LANES, LANES),
            vmem(2, LANES, LANES),
            vmem(8, 8, LANES),
            pltpu.VMEM((4, 128, LANES), jnp.int32),
            dma,
            dma((8,)), dma((8,)), dma((8,)), dma((8,)),
            dma((2,)), dma((2,)), dma((2,)), dma((2,)),
            dma((2, 8)), dma((2, 8)),
            dma((len(EXCHANGED), 8)), dma((len(EXCHANGED), 8)),
            dma, dma,
            dma((9,)), dma((9,)),
            dma((4, 2)), dma((8,)),
            dma, dma((3,)), dma((32,)), dma((8,)),
        ],
        compiler_params=pltpu.CompilerParams(
            collective_id=0, has_side_effects=True, vmem_limit_bytes=60 * 1024 * 1024
        ),
    )(checkpoints, guess, materials, table, weight)
    parts = shares[:, :, :64].reshape(8, 8, 4, 16)
    sensitivity = jnp.transpose(parts, (2, 0, 3, 1)).reshape(4, 128, 8)
    return corrected, sensitivity


def solution(mesh):
    in_specs = (
        P("tm", "space", None, None),
        P("tm", "space", None, None),
        P("space", None, None),
        P(),
        P("space", None, None),
    )
    out_specs = (P("tm", "space", None, None), P("space", None, "tm"))
    return jax.shard_map(
        on_device, mesh=mesh, in_specs=in_specs, out_specs=out_specs, check_vma=False
    )
```

```python
import functools

import jax
import jax.numpy as jnp
from jax import lax
from jax.experimental import pallas as pl
from jax.experimental.pallas import tpu as pltpu
from jax.sharding import PartitionSpec as P

MESH = pl.DeviceIdType.MESH
F32 = jnp.float32

RATE = 0.006
SLOPE = 0.5
LEVELS = 8
Q, PLANES, ROWS, LANES, H = 4, 8, 16, 128, 4
PADP, PADR = PLANES + 2 * H, ROWS + 2 * H
MID_P, MID_R = pl.ds(H, PLANES), pl.ds(0, ROWS)
SIDES = [(-1, 0), (1, 0), (0, -1), (0, 1), (-1, -1), (1, -1), (-1, 1), (1, 1)]
OPPOSITE = [SIDES.index((-dx, -dz)) for dx, dz in SIDES]
RELAX, FINAL, U2, U6 = 8, 9, 17, 18
EXCHANGED = [0, 3, 7, U2, U6, RELAX, RELAX + 4, RELAX + 8, FINAL, FINAL + 4]
SOME = {RELAX + 8: (1, 3), FINAL: (0, 3)}
WIDTH = [3, 1, 2, 3, 0, 1, 2, 3]
PLACE = [(3, 1), (2, 1), (1, 1), (0, 1), (3, 0), (2, 0), (1, 0), (0, 0)]
COEF_W = [3, 2, 1, 3]
CORNER = [(1, 3, 0), (2, 2, 3), (3, 1, 5)]


def rows_of(width):
    return PADR if width else ROWS


def chunks(width):
    lo, hi = H - width, H + PLANES + width
    parts = -(-(hi - lo) // 5)
    edges = [lo + (hi - lo) * n // parts for n in range(parts + 1)]
    return list(zip(edges[:-1], edges[1:]))


def kernel(
    ck, guess, mats, table, weight,
    out, sens_out,
    st, yh, ys, zh_, zs_, c0, c1, c2, c3, base_src, bb, wt, bwh, bws, bzh, bzs, g, cor, err, eyh, eys, ezh, ezs,
    total, turned, sr, s2, sf, ids_, id_sem, own, own_sem,
    ck_send, ck_recv, gu_send, gu_recv, bs_send, bs_recv, wt_send, wt_recv,
    bx_send, bx_recv, ex_send, ex_recv, hop_send, hop_recv,
    ce_send, ce_recv, co_send, co_recv, r1_send, r1_recv, r2_send, r2_recv,
):
    coef = [c0, c1, c2, c3]
    t, s = lax.axis_index("tm"), lax.axis_index("space")
    y, zl, c = t // 4, (t // 2) % 2, t % 2
    x, zh = s // 4, s % 4
    z = zh * 2 + zl
    px = x * 2 + c
    mine = zl * 2 + c
    half = zh % 2

    def dev(px_, y_, z_):
        return {"tm": y_ * 4 + (z_ % 2) * 2 + px_ % 2, "space": (px_ // 2) * 4 + z_ // 2}

    def there(dx, dz):
        ok = jnp.bool_(True)
        if dx:
            ok = px > 0 if dx < 0 else px < 7
        if dz:
            ok_z = z > 0 if dz < 0 else z < 7
            ok = jnp.logical_and(ok, ok_z) if dx else ok_z
        return ok

    near = [(there(dx, dz), px + dx, z + dz) for dx, dz in SIDES]

    barrier = pltpu.get_barrier_semaphore()
    fetch = pltpu.make_async_copy(mats, ids_, id_sem)
    fetch.start()
    slabs = [
        pltpu.make_async_copy(ref, own.at[n], own_sem.at[n])
        for n, ref in enumerate((ck.at[0], guess.at[0], weight))
    ]
    for slab in slabs:
        slab.start()

    def greet(px_, y_, z_):
        pl.semaphore_signal(barrier, inc=1, device_id=dev(px_, y_, z_), device_id_type=MESH)

    def ring(i, carry):
        z_, px_ = i // 2, x * 2 + i % 2

        @pl.when(jnp.logical_or(z_ != z, px_ != px))
        def _():
            greet(px_, y, z_)

        return carry

    lax.fori_loop(0, 16, ring, 0)
    count = jnp.int32(15)
    far_ok = jnp.where(c == 0, px > 0, px < 7)
    far = jnp.where(c == 0, px - 1, px + 1)
    for dz in (-1, 0, 1):
        ok = jnp.logical_and(far_ok, there(0, dz)) if dz else far_ok

        @pl.when(ok)
        def _(dz=dz):
            greet(far, y, z + dz)

        count = count + ok.astype(jnp.int32)

    for dy in range(1, 4):
        greet(px, (y + dy) % 4, z)
    count = count + 3

    @pl.when(y > 0)
    def _():
        for z_ in range(8):
            greet(x * 2 + zh // 2, 0, z_)

    count = count + jnp.where(y == 0, 24, 0)
    for ok, px_, z_ in near:

        @pl.when(jnp.logical_and(ok, y < 3))
        def _(px_=px_, z_=z_):
            greet(px_, y + 1, z_)

        count = count + jnp.logical_and(ok, y > 0).astype(jnp.int32)

    def lookup(p, carry):
        ids = ids_[p]
        val = jnp.zeros(ids.shape, F32)
        for number in range(8):
            val = val + jnp.where(ids == number, table[number], 0.0)
        base_src[p] = val
        return carry

    fetch.wait()
    lax.fori_loop(0, 4, lookup, 0)

    def clear_corners(axis, sign):
        for n in range(4):
            if SIDES[4 + n][axis] == sign:
                tile = jnp.zeros((8, LANES), F32)
                bzh[0, n, 0] = tile
                bzh[1, n, 0] = tile
                ezh[n, 0] = tile

                def clear(q, carry):
                    for e in range(len(EXCHANGED)):
                        zh_[e, n, q] = tile
                    return carry

                lax.fori_loop(0, Q, clear, 0)

    for side, lo in ((0, 0), (1, H + PLANES)):

        @pl.when(jnp.logical_not(near[side][0]))
        def _(side=side, lo=lo):
            slab = jnp.zeros((H, PADR, LANES), F32)
            for ref in (bb, wt, err.at[0]):
                ref[pl.ds(lo, H)] = slab

            def clear(q, carry):
                for idx in EXCHANGED:
                    st[idx, q, pl.ds(lo, H)] = slab
                return carry

            lax.fori_loop(0, Q, clear, 0)
            clear_corners(0, SIDES[side][0])

    for side, k in ((2, 0), (3, 1)):

        @pl.when(jnp.logical_not(near[side][0]))
        def _(side=side, k=k):
            edge = jnp.zeros((32, LANES), F32)
            for n in range(2):
                bwh[n, k, 0] = edge
            eyh[k, 0] = edge

            def clear(q, carry):
                for n in range(len(EXCHANGED)):
                    yh[n, k, q] = edge
                return carry

            lax.fori_loop(0, Q, clear, 0)
            clear_corners(1, SIDES[side][1])

    @pl.when(y == 3)
    def _():
        err[0] = jnp.zeros((PADP, PADR, LANES), F32)
        st[RELAX, 3, MID_P, MID_R] = jnp.zeros((PLANES, ROWS, LANES), F32)

    for slab in slabs:
        slab.wait()
    pl.semaphore_wait(barrier, count)

    def push(src, dst, ssem, rsem, px_, y_, z_):
        here = jnp.logical_and(jnp.logical_and(px_ == px, z_ == z), y_ == y)

        @pl.when(here)
        def _():
            pltpu.make_async_copy(src, dst, rsem).start()

        @pl.when(jnp.logical_not(here))
        def _():
            pltpu.make_async_remote_copy(
                src_ref=src, dst_ref=dst, send_sem=ssem, recv_sem=rsem,
                device_id=dev(px_, y_, z_), device_id_type=MESH,
            ).start()

    def push_done(src, ssem, px_, y_, z_):
        here = jnp.logical_and(jnp.logical_and(px_ == px, z_ == z), y_ == y)

        @pl.when(jnp.logical_not(here))
        def _():
            pltpu.make_async_copy(src, src, ssem).wait()

    def arrived(dst, rsem):
        pltpu.make_async_copy(dst, dst, rsem).wait()

    to_px = x * 2 + zh // 2
    slot = half * 4 + mine

    def cut(ref, z_):
        return ref.at[pl.ds(0, 4), pl.ds(pl.multiple_of(z_ * ROWS, ROWS), ROWS)]

    def turn(i):
        k = (i + 1) // 2
        return (z + jnp.where(i % 2 == 0, 4 + k, 4 - k)) % 8

    def send_ck(i, carry):
        z_ = turn(i)
        push(cut(own.at[0], z_), st.at[0, mine, pl.ds(H + 4 * half, 4), MID_R], ck_send.at[i], ck_recv.at[slot], to_px, y, z_)
        return carry

    def send_guess(i, carry):
        z_ = turn(i)
        push(cut(own.at[1], z_), g.at[mine, pl.ds(4 * half, 4)], gu_send.at[i], gu_recv.at[slot], to_px, y, z_)
        return carry

    for i in range(2):
        z_ = 2 * mine + i
        push(cut(base_src, z_), bb.at[pl.ds(H + 4 * half, 4), MID_R], bs_send.at[i], bs_recv.at[half], to_px, y, z_)
    lax.fori_loop(0, 8, send_ck, 0)

    def outgoing(field, side):
        planes, rows_out, corner_out, _, _ = field
        dx, dz = SIDES[side]
        if dz == 0:
            return planes(H if dx < 0 else PLANES, H)
        return corner_out(side - 4) if dx else rows_out(0 if dz < 0 else 1)

    def landing(field, side):
        planes, _, _, rows_in, corner_in = field
        dx, dz = SIDES[side]
        if dz == 0:
            return planes(0 if dx < 0 else H + PLANES, H)
        return corner_in(side - 4) if dx else rows_in(0 if dz < 0 else 1)

    def halo_copy(field, to, side, ssem, rsem, y_):
        _, px_, z_ = near[side]
        back = OPPOSITE[side]
        return pltpu.make_async_remote_copy(
            src_ref=outgoing(field, side), dst_ref=landing(to, back), send_sem=ssem(side), recv_sem=rsem(back),
            device_id=dev(px_, y_, z_), device_id_type=MESH,
        )

    def halo_start(field, to, ssem, rsem, y_, sides):
        for side in sides:

            @pl.when(near[side][0])
            def _(side=side):
                halo_copy(field, to, side, ssem, rsem, y_).start()

    def halo_sent(field, to, ssem, rsem, y_, sides=range(8)):
        for side in sides:

            @pl.when(near[side][0])
            def _(side=side):
                halo_copy(field, to, side, ssem, rsem, y_).wait_send()

    def halo_landed(field, rsem):
        for side in range(8):

            @pl.when(near[side][0])
            def _(side=side):
                arrived(landing(field, side), rsem(side))

    def pack_corners(block, corner_out):
        for n in range(4):
            dx, dz = SIDES[4 + n]
            for d, m, at in CORNER:
                plane = H + d - 1 if dx < 0 else H + PLANES - d
                row = 0 if dz < 0 else ROWS - m
                corner_out[0][corner_out[1](n, pl.ds(at, m))] = block[0][block[1](plane, pl.ds(row, m))]

    def pack_rows(block, rows_out):
        for p in range(PLANES):
            for k, row in ((0, 0), (1, ROWS - H)):
                rows_out[0][rows_out[1](k, pl.ds(4 * p, 4))] = block[0][block[1](H + p, pl.ds(row, 4))]

    def unpack(block, rows_in, corner_in):
        for p in range(PLANES):
            for k, row in ((0, PADR - H), (1, ROWS)):
                block[0][block[1](H + p, pl.ds(row, 4))] = rows_in[0][rows_in[1](k, pl.ds(4 * p, 4))]
        for n in range(4):
            dx, dz = SIDES[4 + n]
            for d, m, at in CORNER:
                plane = H - d if dx < 0 else H + PLANES - 1 + d
                row = PADR - m if dz < 0 else ROWS
                block[0][block[1](plane, pl.ds(row, m))] = corner_in[0][corner_in[1](n, pl.ds(at, m))]

    def batch(idx):
        n = EXCHANGED.index(idx)
        some = pl.ds(*SOME.get(idx, (0, Q)))
        field = (
            lambda lo, m: st.at[idx, some, pl.ds(lo, m), MID_R],
            lambda k: ys.at[n, k, some],
            lambda k: zs_.at[n, k, some],
            lambda k: yh.at[n, k, some],
            lambda k: zh_.at[n, k, some],
        )
        return n, field, lambda side: ex_send.at[n, side], lambda side: ex_recv.at[n, side]

    def per_q(one, idx=None):
        def body(q, carry):
            one(q)
            return carry

        lo, m = SOME.get(idx, (0, Q))
        lax.fori_loop(lo, lo + m, body, 0)

    def batch_start(idx):
        n, field, ssem, rsem = batch(idx)
        at = lambda q: (lambda k, rows: (n, k, q, rows))
        block = lambda q: (st, lambda p, rows: (idx, q, p, rows))
        per_q(lambda q: pack_corners(block(q), (zs_, at(q))), idx)
        halo_start(field, field, ssem, rsem, y, (4, 5, 6, 7))
        per_q(lambda q: pack_rows(block(q), (ys, at(q))), idx)
        halo_start(field, field, ssem, rsem, y, (2, 3, 0, 1))

    def batch_wait(idx):
        n, field, ssem, rsem = batch(idx)
        halo_landed(field, rsem)
        at = lambda q: (lambda k, rows: (n, k, q, rows))
        per_q(lambda q: unpack((st, lambda p, rows: (idx, q, p, rows)), (yh, at(q)), (zh_, at(q))), idx)

    def batch_sent(idx):
        n, field, ssem, rsem = batch(idx)
        halo_sent(field, field, ssem, rsem, y)

    def static_field(n):
        ref = bb if n == 0 else wt
        field = (
            lambda lo, m: ref.at[pl.ds(lo, m), MID_R],
            lambda k: bws.at[n, k, 0],
            lambda k: bzs.at[n, k, 0],
            lambda k: bwh.at[n, k, 0],
            lambda k: bzh.at[n, k, 0],
        )
        return field, lambda side: bx_send.at[n, side], lambda side: bx_recv.at[n, side]

    def static_start(n):
        ref, sem = (bb, bs_recv) if n == 0 else (wt, wt_recv)
        for i in range(2):
            arrived(ref.at[pl.ds(H + 4 * i, 4), MID_R], sem.at[i])
        at = lambda k, rows: (n, k, 0, rows)
        block = (ref, lambda p, rows: (p, rows))
        pack_corners(block, (bzs, at))
        pack_rows(block, (bws, at))
        field, ssem, rsem = static_field(n)
        halo_start(field, field, ssem, rsem, y, (4, 5, 6, 7, 2, 3, 0, 1))

    def static_wait(n):
        field, ssem, rsem = static_field(n)
        halo_landed(field, rsem)
        at = lambda k, rows: (n, k, 0, rows)
        unpack((bb if n == 0 else wt, lambda p, rows: (p, rows)), (bwh, at), (bzh, at))

    static_start(0)
    for i in range(8):
        arrived(st.at[0, i % 4, pl.ds(H + 4 * (i // 4), 4), MID_R], ck_recv.at[i])
    batch_start(0)
    for i in range(2):
        z_ = 2 * mine + i
        push(cut(own.at[2], z_), wt.at[pl.ds(H + 4 * half, 4), MID_R], wt_send.at[i], wt_recv.at[half], to_px, y, z_)
    static_wait(0)
    batch_wait(0)
    lax.fori_loop(0, 4, send_guess, 0)

    def edges(n, rows):
        lane = lax.broadcasted_iota(jnp.int32, (n, rows, LANES), 2)
        return lane == 0, lane == LANES - 1

    def up(a):
        return pltpu.roll(a, PADR - 1, 1)

    def down(a):
        return pltpu.roll(a, 1, 1)

    def right(a):
        return pltpu.roll(a, LANES - 1, 2)

    def left(a):
        return pltpu.roll(a, 1, 2)

    def forward(j, width, copy=None):
        rows = rows_of(width)

        def one(q):
            for lo, hi in chunks(width):
                n = hi - lo
                first, last = edges(n, rows)
                uu = st[j, q, pl.ds(lo - 1, n + 2)]
                kk = bb[pl.ds(lo - 1, n + 2)] * (1.0 + SLOPE * uu)
                u, k = uu[1:-1], kk[1:-1]
                f = (k + up(k)) * (up(u) - u)
                flow = (f - down(f))[:, :rows]
                uu, kk, u, k = uu[:, :rows], kk[:, :rows], u[:, :rows], k[:, :rows]
                f = (kk[1:] + kk[:-1]) * (uu[1:] - uu[:-1])
                flow = flow + (f[1:] - f[:-1])
                f = (k + jnp.where(last, 0.0, right(k))) * (jnp.where(last, 0.0, right(u)) - u)
                flow = flow + (f - jnp.where(first, k * u, left(f)))
                new = u + (0.5 * RATE) * flow
                if width:
                    new = jnp.where(bb[pl.ds(lo, n)] > 0.0, new, 0.0)
                st[j + 1, q, pl.ds(lo, n), pl.ds(0, rows)] = new
                if copy is not None:
                    a, z_ = max(lo, H), min(hi, H + PLANES)
                    if a < z_:
                        st[copy, q, pl.ds(a, z_ - a), MID_R] = new[a - lo : z_ - lo, :ROWS]

        per_q(one)

    def coefficients(j, field=None):
        idx = j if field is None else field
        array, entry = PLACE[j]
        ref, off = coef[array], H - COEF_W[array]
        rows = rows_of(WIDTH[j])

        def one(q):
            for lo, hi in chunks(WIDTH[j]):
                n = hi - lo
                first, last = edges(n, rows)
                uu = st[idx, q, pl.ds(lo - 1, n + 2)]
                base = bb[pl.ds(lo - 1, n + 2)]
                kk = (0.5 * RATE) * (base * (1.0 + SLOPE * uu))
                u, k = uu[1:-1], kk[1:-1]
                b = (0.25 * RATE) * base[1:-1, :rows]
                at = lambda i: (entry, q, i, pl.ds(lo - off, n), pl.ds(0, rows))
                a, d = k + up(k), up(u) - u
                less, more = down(a)[:, :rows] + b * down(d)[:, :rows], a[:, :rows] - b * d[:, :rows]
                ref[at(3)] = less
                ref[at(4)] = more
                w_sum = less + more
                uu, kk, u, k = uu[:, :rows], kk[:, :rows], u[:, :rows], k[:, :rows]
                a, d = kk[1:] + kk[:-1], uu[1:] - uu[:-1]
                less, more = a[:-1] + b * d[:-1], a[1:] - b * d[1:]
                ref[at(1)] = less
                ref[at(2)] = more
                w_sum = w_sum + (less + more)
                a, d = k + right(k), right(u) - u
                less, more = left(a) + b * left(d), a - b * d
                ref[at(5)] = jnp.where(first, 0.0, less)
                ref[at(6)] = jnp.where(last, 0.0, more)
                edge = k + b * u
                w_sum = w_sum + (jnp.where(first, edge, less) + jnp.where(last, edge, more))
                ref[at(0)] = w_sum

        per_q(one)

    def change(vv, array, entry, q, lo, n, rows):
        ref, off = coef[array], H - COEF_W[array]
        w = lambda i: ref[entry, q, i, pl.ds(lo - off, n), pl.ds(0, rows)]
        acc = down(vv[1:-1])[:, :rows] * w(3)
        acc = acc + up(vv[1:-1])[:, :rows] * w(4)
        vv = vv[:, :rows]
        v = vv[1:-1]
        acc = acc + (vv[:-2] * w(1) + vv[2:] * w(2))
        acc = acc + left(v) * w(5)
        acc = acc + right(v) * w(6)
        return v, acc - v * w(0)

    def field_of(j):
        return {2: U2, 6: U6}.get(j, j)

    def adjoint(idx, j, width):
        array, entry = PLACE[j]
        rows = rows_of(width)
        some = pl.ds(0, rows)

        def one(q):
            for lo, hi in chunks(width):
                n = hi - lo
                at = pl.ds(lo, n)
                v, more = change(st[idx, q, pl.ds(lo - 1, n + 2)], array, entry, q, lo, n, rows)
                new = (v + more) + wt[at, some] * st[field_of(j), q, at, some]
                if width:
                    new = jnp.where(bb[at] > 0.0, new, 0.0)
                st[idx + 1, q, at, some] = new

        per_q(one)

    def hop_copy():
        return pltpu.make_async_remote_copy(
            src_ref=g.at[0], dst_ref=st.at[RELAX, 3, MID_P, MID_R], send_sem=hop_send, recv_sem=hop_recv,
            device_id=dev(px, (y + 3) % 4, z), device_id_type=MESH,
        )

    forward(0, 2)
    forward(1, 1, copy=U2)
    forward(2, 0)
    batch_start(3)
    static_start(1)

    def rest(i, carry):
        return send_guess(i + 4, carry)

    lax.fori_loop(0, 4, rest, 0)
    coefficients(0)
    coefficients(1)
    static_wait(1)
    batch_wait(3)
    batch_start(U2)
    forward(3, 3)
    for i in range(8):
        arrived(g.at[i % 4, pl.ds(4 * (i // 4), 4)], gu_recv.at[i])

    @pl.when(y > 0)
    def _():
        hop_copy().start()

    for q in range(3):
        st[RELAX, q, MID_P, MID_R] = g[q + 1]
    forward(4, 2)
    forward(5, 1, copy=U6)
    forward(6, 0)
    batch_start(7)
    batch_start(U6)

    @pl.when(y < 3)
    def _():
        hop_copy().wait_recv()

    batch_start(RELAX)
    coefficients(5)
    coefficients(4)
    batch_wait(7)
    coefficients(7)
    batch_wait(U6)
    coefficients(6, U6)
    batch_wait(RELAX)
    for i in range(4):
        adjoint(RELAX + i, 7 - i, 3 - i)
    batch_start(RELAX + 4)
    coefficients(3)
    batch_wait(U2)
    coefficients(2, U2)
    batch_wait(RELAX + 4)
    for i in range(4, 8):
        adjoint(RELAX + i, 7 - i, 7 - i)
    batch_start(RELAX + 8)
    batch_wait(RELAX + 8)

    def err_field(i):
        return (
            lambda lo, m: err.at[i, pl.ds(lo, m), MID_R],
            lambda k: eys.at[k, 0],
            lambda k: ezs.at[k, 0],
            lambda k: eyh.at[k, 0],
            lambda k: ezh.at[k, 0],
        )

    cross = (err_field(4), err_field(0), lambda side: ce_send.at[side], lambda side: ce_recv.at[side])

    def block_copy():
        return pltpu.make_async_remote_copy(
            src_ref=err.at[4, MID_P, MID_R], dst_ref=err.at[0, MID_P, MID_R], send_sem=ce_send.at[8], recv_sem=ce_recv.at[8],
            device_id=dev(px, (y + 3) % 4, z), device_id_type=MESH,
        )

    def packed(k, rows):
        return (k, 0, rows)

    def give(q, i, start):
        src = cor.at[q, pl.ds(4 * i, 4)]
        z_, px_ = 2 * (2 * c + i) + q // 2, x * 2 + q % 2
        if start:
            push(src, out.at[0, pl.ds(0, 4), pl.ds(pl.multiple_of(z * ROWS, ROWS), ROWS)], co_send.at[q, i], co_recv.at[z], px_, y, z_)
        else:
            push_done(src, co_send.at[q, i], px_, y, z_)

    @pl.when(y < 3)
    def _():
        halo_landed(cross[1], cross[3])
        block_copy().wait_recv()
        unpack((err, lambda p, rows: (0, p, rows)), (eyh, packed), (ezh, packed))

    def coarse(i):
        q = 3 - i
        array, entry = PLACE[0]
        rows = rows_of(3 - i)
        some = pl.ds(0, rows)
        for lo, hi in chunks(3 - i):
            n = hi - lo
            at = pl.ds(lo, n)
            e, more = change(err[i, pl.ds(lo - 1, n + 2)], array, entry, q, lo, n, rows)
            before = st[RELAX, q - 1, at, some] if q else g[0, pl.ds(lo - H, n)]
            res = st[RELAX + 8, q, at, some] - before
            new = (e + float(LEVELS) * more) + res
            if i < 3:
                new = jnp.where(bb[at] > 0.0, new, 0.0)
            err[i + 1, at, some] = new

    for i in range(3):
        coarse(i)

    @pl.when(y > 0)
    def _():
        coarse(3)
        block = (err, lambda p, rows: (4, p, rows))
        pack_corners(block, (ezs, packed))
        halo_start(*cross, y - 1, (4, 5, 6, 7))
        pack_rows(block, (eys, packed))
        halo_start(*cross, y - 1, (2, 3, 0, 1))
        block_copy().start()

    for q in range(3):
        st[FINAL, q, MID_P, MID_R] = st[RELAX, q, MID_P, MID_R] + err[3 - q, MID_P, MID_R]
    batch_start(FINAL)
    st[FINAL, 3] = st[RELAX, 3] + err[0]

    @pl.when(y == 0)
    def _():
        coarse(3)

    for q in range(4):
        cor[q] = g[q] + err[4 - q, MID_P, MID_R]

    total[...] = jnp.zeros(total.shape, F32)

    def spread(idx, j):
        def one(q):
            for lo, hi in chunks(0):
                n = hi - lo
                first, last = edges(n, ROWS)
                uu = st[field_of(j), q, pl.ds(lo - 1, n + 2)]
                vv = st[idx, q, pl.ds(lo - 1, n + 2)]
                u, v = uu[1:-1], vv[1:-1]
                f = (up(u) - u) * (up(v) - v)
                acc = (f + down(f))[:, :ROWS]
                uu, vv, u, v = uu[:, :ROWS], vv[:, :ROWS], u[:, :ROWS], v[:, :ROWS]
                f = (uu[1:] - uu[:-1]) * (vv[1:] - vv[:-1])
                acc = acc + (f[1:] + f[:-1])
                f = (jnp.where(last, 0.0, right(u)) - u) * (jnp.where(last, 0.0, right(v)) - v)
                acc = acc + (f + jnp.where(first, u * v, left(f)))
                at = pl.ds(lo - H, n)
                total[at] = total[at] - ((0.5 * RATE) * (1.0 + SLOPE * u)) * acc

        per_q(one)

    batch_wait(FINAL)
    batch_sent(RELAX + 4)
    batch_sent(RELAX + 8)
    for i in range(4):
        adjoint(FINAL + i, 7 - i, 3 - i)
    batch_start(FINAL + 4)
    for i in range(4):
        spread(FINAL + i, 7 - i)
    batch_wait(FINAL + 4)
    for q in range(4):
        for k in range(2):
            give(q, k, True)
    for i in range(4, 8):
        if i < 7:
            adjoint(FINAL + i, 7 - i, 7 - i)
        spread(FINAL + i, 7 - i)

    turned[...] = jnp.transpose(total[...].reshape(PLANES * ROWS, LANES))

    def sum_copy():
        return pltpu.make_async_remote_copy(
            src_ref=turned, dst_ref=sr.at[jnp.maximum(y - 1, 0)], send_sem=r1_send, recv_sem=r1_recv.at[jnp.maximum(y - 1, 0)],
            device_id=dev(px, 0, z), device_id_type=MESH,
        )

    def share(n, start):
        y_, i, q = n // 8, (n // 4) % 2, n % 4
        src = s2.at[i, pl.ds(pl.multiple_of(32 * y_ + 8 * q, 8), 8)]
        z_, px_ = 2 * (2 * c + i) + q // 2, x * 2 + q % 2
        if start:
            push(src, sf.at[z], r2_send.at[n], r2_recv.at[z], px_, y_, z_)
        else:
            push_done(src, r2_send.at[n], px_, y_, z_)

    def share_start(n, carry):
        share(n, True)
        return carry

    def share_done(n, carry):
        share(n, False)
        return carry

    @pl.when(y > 0)
    def _():
        sum_copy().start()

    @pl.when(y == 0)
    def _():
        part = turned[...]
        for n in range(3):
            arrived(sr.at[n], r1_recv.at[n])
            part = part + sr[n]
        s2[0] = part
        s2[1] = pltpu.roll(part, 64, 1)
        lax.fori_loop(0, 32, share_start, 0)

    for i in range(8):
        arrived(sf.at[i], r2_recv.at[i])
    sens_out[...] = sf[...]

    @pl.when(y > 0)
    def _():
        sum_copy().wait_send()

    @pl.when(y == 0)
    def _():
        lax.fori_loop(0, 32, share_done, 0)

    for q in range(4):
        for i in range(2):
            give(q, i, False)
    for i in range(8):
        arrived(out.at[0, pl.ds(0, 4), pl.ds(i * ROWS, ROWS)], co_recv.at[i])

    @pl.when(y > 0)
    def _():
        hop_copy().wait_send()
        block_copy().wait_send()
        halo_sent(*cross, y - 1)

    for idx in EXCHANGED:
        if idx not in (RELAX + 4, RELAX + 8):
            batch_sent(idx)
    for n in range(2):
        field, ssem, rsem = static_field(n)
        halo_sent(field, field, ssem, rsem, y)

    for i in range(2):
        z_ = 2 * mine + i
        push_done(cut(base_src, z_), bs_send.at[i], to_px, y, z_)
        push_done(cut(own.at[2], z_), wt_send.at[i], to_px, y, z_)

    def drain(i, carry):
        z_ = turn(i)
        push_done(cut(own.at[0], z_), ck_send.at[i], to_px, y, z_)
        push_done(cut(own.at[1], z_), gu_send.at[i], to_px, y, z_)
        return carry

    lax.fori_loop(0, 8, drain, 0)


def on_device(checkpoints, guess, materials, table, weight):
    dma = pltpu.SemaphoreType.DMA
    vmem = lambda *shape: pltpu.VMEM(shape, F32)
    block = (PLANES, ROWS, LANES)
    corrected, shares = pl.pallas_call(
        kernel,
        out_shape=(
            jax.ShapeDtypeStruct(guess.shape, F32),
            jax.ShapeDtypeStruct((8, 8, LANES), F32),
        ),
        in_specs=[
            pl.BlockSpec(memory_space=pl.ANY),
            pl.BlockSpec(memory_space=pl.ANY),
            pl.BlockSpec(memory_space=pl.ANY),
            pl.BlockSpec(memory_space=pltpu.SMEM),
            pl.BlockSpec(memory_space=pl.ANY),
        ],
        out_specs=(
            pl.BlockSpec(memory_space=pl.ANY),
            pl.BlockSpec(memory_space=pltpu.VMEM),
        ),
        scratch_shapes=[
            vmem(19, Q, PADP, PADR, LANES),
            vmem(len(EXCHANGED), 2, Q, 32, LANES),
            vmem(len(EXCHANGED), 2, Q, 32, LANES),
            vmem(len(EXCHANGED), 4, Q, 8, LANES),
            vmem(len(EXCHANGED), 4, Q, 8, LANES),
            vmem(2, Q, 7, 14, PADR, LANES),
            vmem(2, Q, 7, 12, PADR, LANES),
            vmem(2, Q, 7, 10, PADR, LANES),
            vmem(2, Q, 7, 14, PADR, LANES),
            vmem(4, 128, LANES),
            vmem(PADP, PADR, LANES),
            vmem(PADP, PADR, LANES),
            vmem(2, 2, 1, 32, LANES),
            vmem(2, 2, 1, 32, LANES),
            vmem(2, 4, 1, 8, LANES),
            vmem(2, 4, 1, 8, LANES),
            vmem(Q, *block),
            vmem(Q, *block),
            vmem(5, PADP, PADR, LANES),
            vmem(2, 1, 32, LANES),
            vmem(2, 1, 32, LANES),
            vmem(4, 1, 8, LANES),
            vmem(4, 1, 8, LANES),
            vmem(*block),
            vmem(LANES, LANES),
            vmem(3, LANES, LANES),
            vmem(2, LANES, LANES),
            vmem(8, 8, LANES),
            pltpu.VMEM((4, 128, LANES), jnp.int32),
            dma,
            vmem(3, 4, 128, LANES),
            dma((3,)),
            dma((8,)), dma((8,)), dma((8,)), dma((8,)),
            dma((2,)), dma((2,)), dma((2,)), dma((2,)),
            dma((2, 8)), dma((2, 8)),
            dma((len(EXCHANGED), 8)), dma((len(EXCHANGED), 8)),
            dma, dma,
            dma((9,)), dma((9,)),
            dma((4, 2)), dma((8,)),
            dma, dma((3,)), dma((32,)), dma((8,)),
        ],
        compiler_params=pltpu.CompilerParams(
            collective_id=0, has_side_effects=True, vmem_limit_bytes=60 * 1024 * 1024
        ),
    )(checkpoints, guess, materials, table, weight)
    parts = shares[:, :, :64].reshape(8, 8, 4, 16)
    sensitivity = jnp.transpose(parts, (2, 0, 3, 1)).reshape(4, 128, 8)
    return corrected, sensitivity


def solution(mesh):
    in_specs = (
        P("tm", "space", None, None),
        P("tm", "space", None, None),
        P("space", None, None),
        P(),
        P("space", None, None),
    )
    out_specs = (P("tm", "space", None, None), P("space", None, "tm"))
    return jax.shard_map(
        on_device, mesh=mesh, in_specs=in_specs, out_specs=out_specs, check_vma=False
    )
```
